32 devices in a mesh: phase: 16 (over z, x, core), slab: 2 (over y).
Axes of the slice: x: 2, y: 2, z: 4, core: 2. Of those that a mesh axis runs over, the one named last changes fastest.
Arguments:
- features: bfloat16 [16, 4, 320, 512], P('phase', 'slab'), may hold values from -6 to 6
- conv_weight: bfloat16 [27, 64, 64], replicated, may hold values from -0.15625 to 0.15625
- projection: bfloat16 [2, 64], replicated, may hold values from -0.75 to 0.75
- grad_out: float32 [16, 4, 2, 8, 320], P('phase', 'slab'), may hold values from -6 to 6
- sens: float32 [4, 16, 2, 8, 320], P('slab'), may hold values from -1 to 1
- mask: int32 [16, 4, 320], P('phase'), may hold values 0 or 1
Outputs:
- grad_image: float32 [16, 4, 2, 8, 320], P('phase', 'slab')
- grad_features: bfloat16 [16, 4, 320, 512], P('phase', 'slab')
- grad_weight: float32 [27, 64, 64], replicated
The draws below stay inside these ranges and needn't reach their ends.
All inputs are finite; a program needn't handle non-finite values. No bound on the sum of `mask` on one device may be relied on, other than what follows from the above.
Results may differ from the reference program's by a relative error of at most 0.0051.
Values may be sent and summed in bfloat16 or wider, within the bound.
No kernel may reach another device: no remote copies, remote signals or barrier semaphores. Data moves between devices by JAX's collectives and lax.ppermute only.
A program may use at most 128 MiB of HBM per device.

```python
import math
import jax
import jax.numpy as jnp
from jax import lax

CHANNELS = 64
NY = 320
COILS = 16
XW = 8
PHASES = 16
SLICES = 4


def touch_ends(values, rng, smallest, largest):
    index_at = [jax.random.randint(jax.random.fold_in(rng, axis), (), 0, length) for axis, length in enumerate(values.shape)]
    widest = values.shape.index(max(values.shape))
    beside = index_at[:widest] + [(index_at[widest] + 1) % values.shape[widest]] + index_at[widest + 1:]
    return values.at[tuple(index_at)].set(smallest).at[tuple(beside)].set(largest)


def steps_of(rng, shape, split, low, top_value):
    loudness, own = 1.0, jax.random.fold_in(rng, 6)
    for dim, parts in split:
        steps = jnp.exp(jax.random.uniform(jax.random.fold_in(own, dim), (parts,), jnp.float32, low / len(split), top_value / len(split)))
        loudness = loudness * jnp.repeat(steps, shape[dim] // parts).reshape([-1 if axis == dim else 1 for axis in range(len(shape))])
    return loudness


def centred(rng, extent, width, limit, shards=(), kind=jnp.bfloat16):
    values = width * jax.random.normal(rng, extent, jnp.float32)
    if shards:
        values = values * steps_of(rng, extent, shards, -0.22, 0.18)
    return jnp.clip(values, -limit, limit).astype(kind)


def setup_inputs(seed: int = 0) -> dict:
    streams_of = jax.random.split(jax.random.key(seed), 7)
    features = centred(streams_of[0], (PHASES, SLICES, NY, XW * CHANNELS), 1.0, 6.0, ((0, 16), (1, 2)))
    conv_weight = centred(streams_of[1], (27, CHANNELS, CHANNELS), (27 * CHANNELS) ** -0.5, 0.15625)
    projection = centred(streams_of[2], (2, CHANNELS), CHANNELS ** -0.5, 0.75)
    grad_out = centred(streams_of[3], (PHASES, SLICES, 2, XW, NY), 1.0, 6.0, ((0, 16), (1, 2)), jnp.float32)
    sens = centred(streams_of[4], (SLICES, COILS, 2, XW, NY), 0.18, 1.0, ((0, 2),), jnp.float32)
    mask = touch_ends((jax.random.randint(streams_of[5], (PHASES, SLICES, NY), 0, 3) < 1).astype(jnp.int32), jax.random.fold_in(streams_of[5], 1), 0, 1)
    return {"features": features, "conv_weight": conv_weight, "projection": projection, "grad_out": grad_out, "sens": sens, "mask": mask}


def dft_matrix(length, direction):
    indices = jnp.arange(length, dtype=jnp.int32)
    product = indices[:, None] * indices[None, :] % length
    angles = product.astype(jnp.float32) * (2.0 * math.pi / length)
    scaling = 1.0 / math.sqrt(length)
    cosine = jnp.cos(angles) * scaling
    sine_part = jnp.sin(angles) * (scaling * direction)
    return jnp.stack([jnp.stack([cosine, -sine_part], 1), jnp.stack([sine_part, cosine], 1)], 0)

def along_rows(values, matrix):
    return jnp.einsum('...pxy,pyqk->...qxk', values, matrix, precision=lax.Precision.HIGHEST)

def along_depth(values, matrix):
    return jnp.einsum('tzcpxy,pzqw->twcqxy', values, matrix, precision=lax.Precision.HIGHEST)

def normal_image(image, sens, mask):
    sens_real = sens[:, :, 0]
    sens_imag = sens[:, :, 1]
    img_real = image[:, :, 0][:, :, None]
    img_imag = image[:, :, 1][:, :, None]
    coil_images = jnp.stack([sens_real * img_real - sens_imag * img_imag, sens_real * img_imag + sens_imag * img_real], axis=3)
    kspace = along_rows(coil_images, dft_matrix(NY, 1.0))
    kspace = along_depth(kspace, dft_matrix(SLICES, 1.0))
    kspace = kspace * mask[:, :, None, None, None, :].astype(jnp.float32)
    kspace = along_depth(kspace, dft_matrix(SLICES, -1.0))
    image_back = along_rows(kspace, dft_matrix(NY, -1.0))
    back_real = image_back[:, :, :, 0]
    back_imag = image_back[:, :, :, 1]
    normal_real = lax.optimization_barrier(jnp.sum(sens_real * back_real + sens_imag * back_imag, axis=2))
    normal_imag = lax.optimization_barrier(jnp.sum(sens_real * back_imag - sens_imag * back_real, axis=2))
    return jnp.stack([normal_real, normal_imag], axis=2)

def phase_rows(array5, phase_now, offsets):
    picked = [lax.dynamic_index_in_dim(array5, jnp.mod(phase_now + offset, PHASES).astype(jnp.int32), 0, keepdims=False) for offset in offsets]
    stacked = jnp.stack(picked).astype(jnp.float32)
    return jnp.pad(stacked, ((0, 0), (1, 1), (1, 1), (0, 0), (0, 0)))

def reference(features, conv_weight, projection, grad_out, sens, mask):
    feat5 = features.reshape(PHASES, SLICES, NY, XW, CHANNELS)
    grad_image = grad_out - normal_image(grad_out, sens, mask)
    proj32 = projection.astype(jnp.float32)
    weight32 = conv_weight.astype(jnp.float32)

    def act_grad(phase_now):
        padded = phase_rows(feat5, phase_now, (-1, 0, 1))
        summed = jnp.zeros((SLICES, NY, XW, CHANNELS), jnp.float32)
        for time_off in range(3):
            for depth_off in range(3):
                for row_off in range(3):
                    piece = padded[time_off, depth_off:depth_off + SLICES, row_off:row_off + NY]
                    summed = summed + jnp.einsum('zyxf,fg->zyxg', piece, weight32[9 * time_off + 3 * depth_off + row_off], precision=lax.Precision.HIGHEST)
        image_now = lax.dynamic_index_in_dim(grad_image, phase_now, 0, keepdims=False)
        grad_silu = -jnp.einsum('zcxy,cf->zyxf', image_now, proj32, precision=lax.Precision.HIGHEST)
        sigmoid_act = jax.nn.sigmoid(summed)
        slope = sigmoid_act * (1.0 + summed * (1.0 - sigmoid_act))
        return (grad_silu * slope).astype(jnp.bfloat16)
    grad_act = lax.map(act_grad, jnp.arange(PHASES, dtype=jnp.int32))

    def feat_grad(phase_now):
        padded = phase_rows(grad_act, phase_now, (1, 0, -1))
        summed = jnp.zeros((SLICES, NY, XW, CHANNELS), jnp.float32)
        for time_off in range(3):
            for depth_off in range(3):
                for row_off in range(3):
                    piece = padded[time_off, 2 - depth_off:2 - depth_off + SLICES, 2 - row_off:2 - row_off + NY]
                    summed = summed + jnp.einsum('zyxg,fg->zyxf', piece, weight32[9 * time_off + 3 * depth_off + row_off], precision=lax.Precision.HIGHEST)
        return summed.astype(jnp.bfloat16)
    grad_features = lax.map(feat_grad, jnp.arange(PHASES, dtype=jnp.int32)).reshape(PHASES, SLICES, NY, XW * CHANNELS)

    def weight_step(carry, phase_now):
        padded = phase_rows(feat5, phase_now, (-1, 0, 1))
        grad_now = lax.dynamic_index_in_dim(grad_act, phase_now, 0, keepdims=False).astype(jnp.float32)
        terms = []
        for time_off in range(3):
            for depth_off in range(3):
                for row_off in range(3):
                    piece = padded[time_off, depth_off:depth_off + SLICES, row_off:row_off + NY]
                    terms.append(jnp.einsum('zyxf,zyxg->fg', piece, grad_now, precision=lax.Precision.HIGHEST))
        return (carry + jnp.stack(terms), None)
    grad_weight, unused = lax.scan(weight_step, jnp.zeros((27, CHANNELS, CHANNELS), jnp.float32), jnp.arange(PHASES, dtype=jnp.int32))
    return (grad_image, grad_features, grad_weight)
```

```python
import functools
import math

import jax
import jax.numpy as jnp
import ml_dtypes
import numpy as np
from jax import lax
from jax.experimental import pallas as pl
from jax.experimental.pallas import tpu as pltpu
from jax.sharding import PartitionSpec as P

F32, BF16 = jnp.float32, jnp.bfloat16
VMEM = pl.BlockSpec(memory_space=pltpu.VMEM)
SMEM = pl.BlockSpec(memory_space=pltpu.SMEM)
LIMIT = 48 * 1024 * 1024
LANES = 128


def call(body, outs, n_in, n_smem=0, scratch=(), flops=0, nbytes=0):
    return pl.pallas_call(
        body,
        out_shape=outs,
        in_specs=[SMEM] * n_smem + [VMEM] * n_in,
        out_specs=jax.tree.map(lambda _: VMEM, outs),
        scratch_shapes=list(scratch),
        compiler_params=pltpu.CompilerParams(vmem_limit_bytes=LIMIT),
        cost_estimate=pl.CostEstimate(flops=flops, bytes_accessed=nbytes, transcendentals=0),
    )


def dft_packed(length):
    full = length // LANES * LANES
    part = np.concatenate([np.zeros(full), np.ones(full), np.zeros(length - full), np.ones(length - full)])
    index = np.concatenate([np.arange(full)] * 2 + [np.arange(full, length)] * 2)
    angle = (index[:, None] * index[None, :] % length) * (2.0 * math.pi / length)
    cosine, sine = np.cos(angle), np.sin(angle)
    same = part[:, None] == part[None, :]
    matrix = np.where(same, cosine, np.where(part[:, None] == 0, -sine, sine)) / math.sqrt(length)
    high = matrix.astype(ml_dtypes.bfloat16)
    low = (matrix - high.astype(np.float64)).astype(ml_dtypes.bfloat16)
    return high, low


def split(value):
    high = value.astype(BF16)
    return high, (value - high.astype(F32)).astype(BF16)


def dot3(high, low, mat_high, mat_low, dims):
    dot = functools.partial(lax.dot_general, dimension_numbers=(dims, ((), ())), preferred_element_type=F32)
    return dot(high, mat_high) + (dot(high, mat_low) + dot(low, mat_high))


def coil_forward_body(grad_ref, sens_ref, high_ref, low_ref, out_ref, send_ref, x_high, x_low):
    depth_len, coils, _, col_len, row_len = sens_ref.shape
    full = row_len // LANES * LANES
    count = coils * col_len
    for z in range(depth_len):
        sens_r, sens_i = sens_ref[z, :, 0], sens_ref[z, :, 1]
        img_r, img_i = grad_ref[z, 0][None], grad_ref[z, 1][None]
        real = sens_r * img_r - sens_i * img_i
        imag = sens_r * img_i + sens_i * img_r
        rest = jnp.concatenate([real[..., full:], imag[..., full:]], axis=-1)
        for piece, start in ((real[..., :full], 0), (imag[..., :full], full), (rest, 2 * full)):
            width = piece.shape[-1]
            high, low = split(piece.reshape(count, width))
            x_high[z * count : (z + 1) * count, start : start + width] = high
            x_low[z * count : (z + 1) * count, start : start + width] = low
    result = dot3(x_high[...], x_low[...], high_ref[...], low_ref[...], ((1,), (0,)))
    out_ref[...] = result
    send_ref[...] = result.astype(BF16)


def coil_backward_body(slabs, grad_ref, sens_ref, mask_ref, high_ref, low_ref, own_ref, *refs):
    others, out_ref, x_high, x_low = refs[: slabs - 1], refs[-3], refs[-2], refs[-1]
    depth_len, coils, _, col_len, row_len = sens_ref.shape
    total = slabs * depth_len
    full = row_len // LANES * LANES
    rem = row_len - full
    count = coils * col_len
    mask = mask_ref[...].astype(F32)

    def table(turn):
        real = jnp.zeros((1, row_len), F32)
        imag = jnp.zeros((1, row_len), F32)
        has_imag = False
        for kz in range(total):
            angle = 2.0 * math.pi * ((kz * turn) % total) / total
            cosine, sine = round(math.cos(angle), 15) / total, round(math.sin(angle), 15) / total
            real = real + mask[kz : kz + 1] * cosine
            if sine != 0.0:
                imag = imag + mask[kz : kz + 1] * sine
                has_imag = True
        real_rest = jnp.concatenate([real[:, full:], real[:, full:]], axis=-1)
        imag_rest = jnp.concatenate([-imag[:, full:], imag[:, full:]], axis=-1)
        return real[:, :full], imag[:, :full], real_rest, imag_rest, has_imag

    tables = {}
    for z in range(depth_len):
        sums = None
        for step in range(slabs):
            src = own_ref if step == 0 else others[step - 1]
            for zin in range(depth_len):
                turn = (step * depth_len + z - zin) % total
                if turn not in tables:
                    tables[turn] = table(turn)
                real, imag, real_rest, imag_rest, has_imag = tables[turn]
                block = src[zin * count : (zin + 1) * count, :].astype(F32)
                v_r, v_i, v_rest = block[:, :full], block[:, full : 2 * full], block[:, 2 * full :]
                if has_imag:
                    terms = (
                        real * v_r - imag * v_i,
                        real * v_i + imag * v_r,
                        real_rest * v_rest + imag_rest * pltpu.roll(v_rest, rem, 1),
                    )
                else:
                    terms = (real * v_r, real * v_i, real_rest * v_rest)
                sums = terms if sums is None else tuple(a + b for a, b in zip(sums, terms))
        for piece, start in zip(sums, (0, full, 2 * full)):
            high, low = split(piece)
            x_high[z * count : (z + 1) * count, start : start + piece.shape[1]] = high
            x_low[z * count : (z + 1) * count, start : start + piece.shape[1]] = low
    back = dot3(x_high[...], x_low[...], high_ref[...], low_ref[...], ((1,), (1,)))
    for z in range(depth_len):
        sens_r, sens_i = sens_ref[z, :, 0], sens_ref[z, :, 1]
        block = back[z * count : (z + 1) * count].reshape(coils, col_len, 2 * row_len)
        b_r, b_i, b_rest = block[..., :full], block[..., full : 2 * full], block[..., 2 * full :]
        s_r, s_i = sens_r[..., :full], sens_i[..., :full]
        out_ref[z, 0, :, :full] = grad_ref[z, 0, :, :full] - jnp.sum(s_r * b_r + s_i * b_i, axis=0)
        out_ref[z, 1, :, :full] = grad_ref[z, 1, :, :full] - jnp.sum(s_r * b_i - s_i * b_r, axis=0)
        s_rest = jnp.concatenate([sens_r[..., full:], sens_i[..., full:]], axis=-1)
        turned = pltpu.roll(b_rest, rem, 2)
        along = jnp.sum(s_rest * b_rest, axis=0)
        across = jnp.sum(s_rest * turned, axis=0)
        real = along + pltpu.roll(along, rem, 1)
        imag = across - pltpu.roll(across, rem, 1)
        out_ref[z, 0, :, full:] = grad_ref[z, 0, :, full:] - real[:, :rem]
        out_ref[z, 1, :, full:] = grad_ref[z, 1, :, full:] - imag[:, :rem]


def tap_group(scal_ref, phase_kind, flip, step_z):
    core = scal_ref[1]
    time_off = {"own": 1, "on": 2 - 2 * core, "off": 2 * core}[phase_kind]
    depth_off = jnp.where(scal_ref[0] == 1, 2 - step_z, step_z) if flip else step_z
    return 9 * time_off + 3 * depth_off


def shift_rows(value, step):
    rows = value.shape[0]
    turned = pltpu.roll(value, step % rows, 0)
    place = lax.broadcasted_iota(jnp.int32, value.shape, 0)
    return jnp.where(place == (0 if step > 0 else rows - 1), 0.0, turned)


def fill_band(scal_ref, weight_ref, band, entries, outs, flip):
    width = LANES * len(outs)
    for i, (kind, place) in enumerate(entries):
        for j, out_place in enumerate(outs):
            step_z = place - out_place + 1
            for dy in range(3):
                lanes = slice(dy * width + j * LANES, dy * width + (j + 1) * LANES)
                if 0 <= step_z <= 2:
                    block = weight_ref[tap_group(scal_ref, kind, flip, step_z) + dy]
                else:
                    block = jnp.zeros((LANES, LANES), BF16)
                band[i * LANES : (i + 1) * LANES, lanes] = block


def conv_columns(refs, band, lanes):
    stacked = jnp.concatenate([ref[:, lanes] for ref in refs], axis=1)
    taps = jnp.dot(stacked, band[...], preferred_element_type=F32)
    width = taps.shape[1] // 3
    return (
        shift_rows(taps[:, :width], 1)
        + taps[:, width : 2 * width]
        + shift_rows(taps[:, 2 * width :], -1)
    )


def conv_main_body(entries, outs, flip, scal_ref, weight_ref, *refs):
    inputs, out_ref, band = refs[: len(entries)], refs[-2], refs[-1]
    fill_band(scal_ref, weight_ref, band, entries, outs, flip)
    for start in range(0, out_ref.shape[2], LANES):
        lanes = slice(start, start + LANES)
        result = conv_columns(inputs, band, lanes)
        for j in range(len(outs)):
            out_ref[j, :, lanes] = result[:, j * LANES : (j + 1) * LANES]


def corner_sum(groups, scal_ref, weight_ref, refs, bands, flip):
    at = 0
    plans = {}
    for group, ((entries, out_place), band) in enumerate(zip(groups, bands)):
        fill_band(scal_ref, weight_ref, band, entries, (out_place,), flip)
        plans[out_place] = (refs[at : at + len(entries)], band)
        at += len(entries)
    return plans


def grad_act_body(groups, flip, scal_ref, weight_ref, acc_ref, image_ref, spread_ref, *refs):
    n_in = sum(len(entries) for entries, _ in groups)
    inputs, rest = refs[:n_in], refs[n_in:]
    outs = rest[: acc_ref.shape[0]]
    plans = corner_sum(groups, scal_ref, weight_ref, inputs, rest[len(outs) :], flip)
    row_len = image_ref.shape[3]
    for j, out_ref in enumerate(outs):
        place = jnp.where(scal_ref[0] == 1, len(outs) - 1 - j, j) if flip else j
        image = image_ref[place].reshape(-1, row_len)
        first, low = split(image)
        middle, last = split(image - first.astype(F32))
        stacked = jnp.concatenate([first, middle, last], axis=0)
        for start in range(0, acc_ref.shape[2], LANES):
            lanes = slice(start, start + LANES)
            grad_silu = lax.dot_general(
                stacked, spread_ref[:, lanes], (((0,), (0,)), ((), ())), preferred_element_type=F32
            )
            act = acc_ref[j, :, lanes]
            if j in plans:
                act = act + conv_columns(*plans[j], lanes)
            gate = 0.5 * jnp.tanh(0.5 * act) + 0.5
            out_ref[:, lanes] = (grad_silu * (gate * (1.0 + act * (1.0 - gate)))).astype(BF16)


def grad_feature_body(groups, flip, scal_ref, weight_ref, acc_ref, *refs):
    n_in = sum(len(entries) for entries, _ in groups)
    inputs, out_ref, bands = refs[:n_in], refs[n_in], refs[n_in + 1 :]
    plans = corner_sum(groups, scal_ref, weight_ref, inputs, bands, flip)
    depth_len = acc_ref.shape[0]
    for j in range(depth_len):
        place = jnp.where(scal_ref[0] == 1, depth_len - 1 - j, j) if flip else j
        for start in range(0, acc_ref.shape[2], LANES):
            lanes = slice(start, start + LANES)
            total = acc_ref[j, :, lanes]
            if j in plans:
                total = total + conv_columns(*plans[j], lanes)
            out_ref[place, :, lanes] = total.astype(BF16)


def grad_weight_body(entries, outs, flip, scal_ref, *refs):
    n_in, n_out = len(entries), len(outs)
    inputs, grads = refs[:n_in], refs[n_in : n_in + n_out]
    keep_ref, send_ref, left, right, packed = refs[n_in + n_out :]
    rows, packed_len = inputs[0].shape
    half = LANES // 2
    width = LANES * n_out
    for i, start in enumerate(range(0, packed_len, LANES)):
        lanes = slice(start, start + LANES)
        span = slice(i * rows, (i + 1) * rows)
        for k, ref in enumerate(inputs):
            left[span, k * LANES : (k + 1) * LANES] = ref[:, lanes]
        for j, ref in enumerate(grads):
            value = ref[:, lanes].astype(F32)
            right[span, j * LANES : (j + 1) * LANES] = shift_rows(value, -1).astype(BF16)
            right[span, width + j * LANES : width + (j + 1) * LANES] = ref[:, lanes]
            right[span, 2 * width + j * LANES : 2 * width + (j + 1) * LANES] = shift_rows(value, 1).astype(BF16)
    product = lax.dot_general(left[...], right[...], (((0,), (0,)), ((), ())), preferred_element_type=F32)
    lane = lax.broadcasted_iota(jnp.int32, (half // 2, LANES), 1)
    packed[27 * half // 2 :] = jnp.zeros((packed.shape[0] - 27 * half // 2, LANES), F32)
    quarter = half // 2
    for kind in ("own", "on", "off"):
        for step_z in range(3):
            for dy in range(3):
                total = None
                for k, (this, place) in enumerate(entries):
                    for j, out_place in enumerate(outs):
                        if this == kind and place - out_place + 1 == step_z:
                            block = product[
                                k * LANES : (k + 1) * LANES,
                                dy * width + j * LANES : dy * width + (j + 1) * LANES,
                            ]
                            total = block if total is None else total + block
                direct = jnp.where(lane < half, total[:quarter], total[3 * quarter :])
                turned = jnp.where(lane < half, total[quarter : 2 * quarter], total[2 * quarter : 3 * quarter])
                tap = tap_group(scal_ref, kind, flip, step_z) + dy
                packed[pl.ds(pl.multiple_of(tap * quarter, quarter), quarter), :] = direct + pltpu.roll(turned, half, 1)
    share = packed.shape[0] // 2
    core = scal_ref[1]
    keep_ref[...] = packed[pl.ds(pl.multiple_of(core * share, quarter), share), :]
    send_ref[...] = packed[pl.ds(pl.multiple_of((1 - core) * share, quarter), share), :]


def unpack_body(where_ref, *refs):
    pieces, out_ref, packed = refs[:-2], refs[-2], refs[-1]
    share = pieces[0].shape[0]
    for i, ref in enumerate(pieces):
        packed[where_ref[i]] = ref[...].astype(F32)
    flat = packed[...].reshape(-1, LANES)
    taps, height, _ = out_ref.shape
    quarter = height // 2
    for tap in range(taps):
        block = flat[tap * quarter : (tap + 1) * quarter]
        out_ref[tap, :quarter, :] = block[:, : LANES // 2]
        out_ref[tap, quarter:, :] = pltpu.roll(block, LANES // 2, 1)[:, : LANES // 2]


def pair_on(size):
    return [(i, i ^ 1) for i in range(size)]


def pair_off(size):
    return [(i, (i - 1) % size if i % 2 == 0 else (i + 1) % size) for i in range(size)]


def sum_over_mesh(keep, send, phases, slabs):
    phase, slab = lax.axis_index("phase"), lax.axis_index("slab")
    core, column, level = phase % 2, phase // 2 % 2, phase // 4
    both = ("phase", "slab")
    summed = keep + lax.ppermute(send, "phase", pair_on(phases))
    groups = 2 * slabs
    chunks = summed.reshape(groups, summed.shape[0] // groups, LANES)

    def moves(dx, ds):
        return [
            (p * slabs + s, (p ^ (2 * dx)) * slabs + (s + ds) % slabs) for p in range(phases) for s in range(slabs)
        ]

    offsets = [(dx, ds) for dx in range(2) for ds in range(slabs) if (dx, ds) != (0, 0)]
    place = lambda dx, ds: (column ^ dx) * slabs + (slab + ds) % slabs
    part = lax.dynamic_index_in_dim(chunks, place(0, 0), 0, keepdims=False)
    arrived = [
        lax.ppermute(lax.dynamic_index_in_dim(chunks, place(dx, ds), 0, keepdims=False), both, moves(dx, ds))
        for dx, ds in offsets
    ]
    for value in arrived:
        part = part + value
    levels = phases // 4
    arrived = [
        lax.ppermute(part, "phase", [(p, (p + 4 * k) % phases) for p in range(phases)]) for k in range(1, levels)
    ]
    for value in arrived:
        part = part + value
    part = part.astype(BF16)
    pieces, where = [part], [place(0, 0)]
    for dx, ds in offsets:
        pieces.append(lax.ppermute(part, both, moves(dx, ds)))
        where.append(place(dx, -ds))
    other = [lax.ppermute(piece, "phase", pair_on(phases)) for piece in pieces]
    spots = jnp.stack([core * groups + w for w in where] + [(1 - core) * groups + w for w in where])
    return pieces + other, spots.astype(jnp.int32)


def local(phases, slabs, features, conv_weight, projection, grad_out, sens, mask):
    _, depth_len, row_len, packed_len = features.shape
    channels = conv_weight.shape[1]
    col_len = packed_len // channels
    coils = sens.shape[1]
    taps = conv_weight.shape[0]
    slab, core = lax.axis_index("slab"), lax.axis_index("phase") % 2
    flip = slabs == 2
    scal = jnp.stack([slab, core]).astype(jnp.int32)
    on, off = pair_on(phases), pair_off(phases)

    def pass_phase(value, perm):
        return lax.ppermute(value, "phase", perm)

    if flip:
        order = list(range(depth_len))
        edges = [(depth_len - 1, depth_len, [(0, 1), (1, 0)])]
        pick = lambda j: jnp.where(slab == 1, depth_len - 1 - j, j)
    else:
        order = list(range(depth_len))
        up = [(i, i + 1) for i in range(slabs - 1)]
        edges = [(depth_len - 1, -1, up), (0, depth_len, [(j, i) for i, j in up])]
        pick = lambda j: j

    def halo(own):
        off_in = {}
        for j in [edge[0] for edge in edges] + [j for j in order if all(j != edge[0] for edge in edges)]:
            off_in[j] = pass_phase(own[j], off)
        slab_in = [lax.ppermute(own[edge[0]], "slab", edge[2]) for edge in edges]
        on_in = [pass_phase(own[j], on) for j in order]
        corner_off = [lax.ppermute(off_in[edge[0]], "slab", edge[2]) for edge in edges]
        corner_on = [pass_phase(value, on) for value in slab_in]
        main = list(own) + slab_in + on_in + [off_in[j] for j in order]
        corners = []
        for a, b in zip(corner_off, corner_on):
            corners += [a, b]
        return main, corners

    main_entries = (
        [("own", j) for j in order]
        + [("own", edge[1]) for edge in edges]
        + [("on", j) for j in order]
        + [("off", j) for j in order]
    )
    corner_entries = []
    corner_groups = []
    for edge in edges:
        near = min(max(edge[1], 0), depth_len - 1)
        corner_groups.append(([("off", edge[1]), ("on", edge[1])], near))
        corner_entries += [("off", edge[1]), ("on", edge[1])]
    corner_groups.sort(key=lambda g: g[1])

    own_features = [lax.dynamic_index_in_dim(features[0], pick(j), 0, keepdims=False) for j in order]
    main_in, corner_in = halo(own_features)

    high, low = dft_packed(row_len)
    high, low = jnp.asarray(high), jnp.asarray(low)
    lines = depth_len * coils * col_len
    grad_now = grad_out[0]
    line_shape = (lines, 2 * row_len)
    scratch = [pltpu.VMEM(line_shape, BF16)] * 2
    coil_flops = 3 * 2 * lines * (2 * row_len) ** 2
    own_lines, sent_lines = call(
        coil_forward_body,
        (jax.ShapeDtypeStruct(line_shape, F32), jax.ShapeDtypeStruct(line_shape, BF16)),
        4,
        scratch=scratch,
        flops=coil_flops,
        nbytes=4000000,
    )(grad_now, sens, high, low)
    other_lines = [
        lax.ppermute(sent_lines, "slab", [(i, (i + k) % slabs) for i in range(slabs)]) for k in range(1, slabs)
    ]
    grad_image = call(
        functools.partial(coil_backward_body, slabs),
        jax.ShapeDtypeStruct(grad_now.shape, F32),
        6 + len(other_lines),
        scratch=scratch,
        flops=coil_flops,
        nbytes=5000000,
    )(grad_now, sens, mask[0], high, low, own_lines, *other_lines)

    def two_columns(weight):
        zero = jnp.zeros_like(weight)
        return jnp.concatenate(
            [jnp.concatenate([weight, zero], axis=2), jnp.concatenate([zero, weight], axis=2)], axis=1
        )

    weight_forward = two_columns(conv_weight)
    weight_backward = two_columns(jnp.swapaxes(conv_weight[::-1], 1, 2))
    spread = -(projection[:, None, None, :] * jnp.eye(col_len, dtype=BF16)[None, :, :, None])
    spread = spread.reshape(2 * col_len, packed_len)
    spread = jnp.concatenate([spread] * 3, axis=0)

    slice_shape = (row_len, packed_len)
    slab_shape = (depth_len, row_len, packed_len)
    conv_flops = 2 * row_len * len(main_entries) * packed_len * 3 * depth_len * LANES
    bands = [pltpu.VMEM((len(g[0]) * LANES, 3 * LANES), BF16) for g in corner_groups]
    small_flops = 2 * row_len * 2 * packed_len * 3 * LANES

    def conv_main(weight, inputs):
        return call(
            functools.partial(conv_main_body, main_entries, tuple(order), flip),
            jax.ShapeDtypeStruct(slab_shape, F32),
            1 + len(inputs),
            1,
            scratch=[pltpu.VMEM((len(inputs) * LANES, 3 * depth_len * LANES), BF16)],
            flops=conv_flops,
            nbytes=5000000,
        )(scal, weight, *inputs)

    def sorted_corners(values):
        if flip:
            return values
        return values[:2] + values[2:]

    acc = conv_main(weight_forward, main_in)
    grad_act = call(
        functools.partial(grad_act_body, corner_groups, flip),
        [jax.ShapeDtypeStruct(slice_shape, BF16)] * depth_len,
        4 + len(corner_in),
        1,
        scratch=bands,
        flops=small_flops,
        nbytes=4000000,
    )(scal, weight_forward, acc, grad_image, spread, *sorted_corners(corner_in))

    main_grad, corner_grad = halo(grad_act)

    share = (taps + 1) // 2 * channels // 2
    keep, send = call(
        functools.partial(grad_weight_body, main_entries + corner_entries, tuple(order), flip),
        [jax.ShapeDtypeStruct((share, LANES), F32)] * 2,
        len(main_in) + len(corner_in) + depth_len,
        1,
        scratch=[
            pltpu.VMEM((packed_len // LANES * row_len, (len(main_in) + len(corner_in)) * LANES), BF16),
            pltpu.VMEM((packed_len // LANES * row_len, 3 * depth_len * LANES), BF16),
            pltpu.VMEM((2 * share, LANES), F32),
        ],
        flops=conv_flops,
        nbytes=5000000,
    )(scal, *main_in, *corner_in, *grad_act)
    pieces, spots = sum_over_mesh(keep, send, phases, slabs)

    acc_back = conv_main(weight_backward, main_grad)
    grad_features = call(
        functools.partial(grad_feature_body, corner_groups, flip),
        jax.ShapeDtypeStruct(slab_shape, BF16),
        2 + len(corner_grad),
        1,
        scratch=bands,
        flops=small_flops,
        nbytes=4000000,
    )(scal, weight_backward, acc_back, *sorted_corners(corner_grad))

    grad_weight = call(
        unpack_body,
        jax.ShapeDtypeStruct(conv_weight.shape, F32),
        len(pieces),
        1,
        scratch=[pltpu.VMEM((len(pieces),) + pieces[0].shape, F32)],
        nbytes=1000000,
    )(spots, *pieces)
    return (grad_image[None], grad_features[None], grad_weight)


def solution(mesh):
    in_specs = (
        P("phase", "slab", None, None),
        P(),
        P(),
        P("phase", "slab", None, None, None),
        P("slab", None, None, None, None),
        P("phase", None, None),
    )
    out_specs = (P("phase", "slab", None, None, None), P("phase", "slab", None, None), P())
    body = functools.partial(local, mesh.shape["phase"], mesh.shape["slab"])
    return jax.shard_map(body, mesh=mesh, in_specs=in_specs, out_specs=out_specs, check_vma=False)
```

```python
import functools
import math

import jax
import jax.numpy as jnp
import ml_dtypes
import numpy as np
from jax import lax
from jax.experimental import pallas as pl
from jax.experimental.pallas import tpu as pltpu
from jax.sharding import PartitionSpec as P

F32, BF16 = jnp.float32, jnp.bfloat16
VMEM = pl.BlockSpec(memory_space=pltpu.VMEM)
SMEM = pl.BlockSpec(memory_space=pltpu.SMEM)
LIMIT = 48 * 1024 * 1024
LANES = 128


ANY = pl.BlockSpec(memory_space=pl.ANY)
SPECS = {"S": SMEM, "V": VMEM, "M": VMEM}


def call(name, body, outs, ins, kinds, scratch=(), flops=0, nbytes=0, after=()):
    count, waits = len(ins), len(after)

    def run(*refs):
        body(*refs[:count], *refs[count + waits :])

    ins = [pltpu.with_memory_space_constraint(x, pltpu.VMEM) if kind == "M" else x for x, kind in zip(ins, kinds)]
    return pl.pallas_call(
        run,
        out_shape=outs,
        in_specs=[SPECS[kind] for kind in kinds] + [ANY] * waits,
        out_specs=[VMEM] * len(outs) if isinstance(outs, (list, tuple)) else VMEM,
        scratch_shapes=list(scratch),
        compiler_params=pltpu.CompilerParams(vmem_limit_bytes=LIMIT),
        cost_estimate=pl.CostEstimate(flops=flops, bytes_accessed=nbytes, transcendentals=0),
        name=name,
    )(*ins, *after)


def dft_packed(length):
    full = length // LANES * LANES
    part = np.concatenate([np.zeros(full), np.ones(full), np.zeros(length - full), np.ones(length - full)])
    index = np.concatenate([np.arange(full)] * 2 + [np.arange(full, length)] * 2)
    angle = (index[:, None] * index[None, :] % length) * (2.0 * math.pi / length)
    cosine, sine = np.cos(angle), np.sin(angle)
    same = part[:, None] == part[None, :]
    matrix = np.where(same, cosine, np.where(part[:, None] == 0, -sine, sine)) / math.sqrt(length)
    high = matrix.astype(ml_dtypes.bfloat16)
    low = (matrix - high.astype(np.float64)).astype(ml_dtypes.bfloat16)
    return high, low


def split(value):
    high = value.astype(BF16)
    return high, (value - high.astype(F32)).astype(BF16)


def dot3(high, low, mat_high, mat_low, dims):
    dot = functools.partial(lax.dot_general, dimension_numbers=(dims, ((), ())), preferred_element_type=F32)
    return dot(high, mat_high) + (dot(high, mat_low) + dot(low, mat_high))


def coil_forward_body(grad_ref, sens_ref, high_ref, low_ref, out_ref, send_ref, x_high, x_low):
    depth_len, coils, _, col_len, row_len = sens_ref.shape
    full = row_len // LANES * LANES
    count = coils * col_len
    for z in range(depth_len):
        sens_r, sens_i = sens_ref[z, :, 0], sens_ref[z, :, 1]
        img_r, img_i = grad_ref[z, 0][None], grad_ref[z, 1][None]
        real = sens_r * img_r - sens_i * img_i
        imag = sens_r * img_i + sens_i * img_r
        rest = jnp.concatenate([real[..., full:], imag[..., full:]], axis=-1)
        for piece, start in ((real[..., :full], 0), (imag[..., :full], full), (rest, 2 * full)):
            width = piece.shape[-1]
            high, low = split(piece.reshape(count, width))
            x_high[z * count : (z + 1) * count, start : start + width] = high
            x_low[z * count : (z + 1) * count, start : start + width] = low
    result = dot3(x_high[...], x_low[...], high_ref[...], low_ref[...], ((1,), (0,)))
    out_ref[...] = result
    send_ref[...] = result.astype(BF16)


def coil_backward_body(slabs, grad_ref, sens_ref, mask_ref, high_ref, low_ref, own_ref, *refs):
    others, out_ref, x_high, x_low = refs[: slabs - 1], refs[-3], refs[-2], refs[-1]
    depth_len, coils, _, col_len, row_len = sens_ref.shape
    total = slabs * depth_len
    full = row_len // LANES * LANES
    rem = row_len - full
    count = coils * col_len
    mask = mask_ref[...].astype(F32)

    def table(turn):
        real = jnp.zeros((1, row_len), F32)
        imag = jnp.zeros((1, row_len), F32)
        has_imag = False
        for kz in range(total):
            angle = 2.0 * math.pi * ((kz * turn) % total) / total
            cosine, sine = round(math.cos(angle), 15) / total, round(math.sin(angle), 15) / total
            real = real + mask[kz : kz + 1] * cosine
            if sine != 0.0:
                imag = imag + mask[kz : kz + 1] * sine
                has_imag = True
        real_rest = jnp.concatenate([real[:, full:], real[:, full:]], axis=-1)
        imag_rest = jnp.concatenate([-imag[:, full:], imag[:, full:]], axis=-1)
        return real[:, :full], imag[:, :full], real_rest, imag_rest, has_imag

    tables = {}
    for z in range(depth_len):
        sums = None
        for step in range(slabs):
            src = own_ref if step == 0 else others[step - 1]
            for zin in range(depth_len):
                turn = (step * depth_len + z - zin) % total
                if turn not in tables:
                    tables[turn] = table(turn)
                real, imag, real_rest, imag_rest, has_imag = tables[turn]
                block = src[zin * count : (zin + 1) * count, :].astype(F32)
                v_r, v_i, v_rest = block[:, :full], block[:, full : 2 * full], block[:, 2 * full :]
                if has_imag:
                    terms = (
                        real * v_r - imag * v_i,
                        real * v_i + imag * v_r,
                        real_rest * v_rest + imag_rest * pltpu.roll(v_rest, rem, 1),
                    )
                else:
                    terms = (real * v_r, real * v_i, real_rest * v_rest)
                sums = terms if sums is None else tuple(a + b for a, b in zip(sums, terms))
        for piece, start in zip(sums, (0, full, 2 * full)):
            high, low = split(piece)
            x_high[z * count : (z + 1) * count, start : start + piece.shape[1]] = high
            x_low[z * count : (z + 1) * count, start : start + piece.shape[1]] = low
    back = dot3(x_high[...], x_low[...], high_ref[...], low_ref[...], ((1,), (1,)))
    for z in range(depth_len):
        sens_r, sens_i = sens_ref[z, :, 0], sens_ref[z, :, 1]
        block = back[z * count : (z + 1) * count].reshape(coils, col_len, 2 * row_len)
        b_r, b_i, b_rest = block[..., :full], block[..., full : 2 * full], block[..., 2 * full :]
        s_r, s_i = sens_r[..., :full], sens_i[..., :full]
        out_ref[z, 0, :, :full] = grad_ref[z, 0, :, :full] - jnp.sum(s_r * b_r + s_i * b_i, axis=0)
        out_ref[z, 1, :, :full] = grad_ref[z, 1, :, :full] - jnp.sum(s_r * b_i - s_i * b_r, axis=0)
        s_rest = jnp.concatenate([sens_r[..., full:], sens_i[..., full:]], axis=-1)
        turned = pltpu.roll(b_rest, rem, 2)
        along = jnp.sum(s_rest * b_rest, axis=0)
        across = jnp.sum(s_rest * turned, axis=0)
        real = along + pltpu.roll(along, rem, 1)
        imag = across - pltpu.roll(across, rem, 1)
        out_ref[z, 0, :, full:] = grad_ref[z, 0, :, full:] - real[:, :rem]
        out_ref[z, 1, :, full:] = grad_ref[z, 1, :, full:] - imag[:, :rem]


def tap_group(scal_ref, phase_kind, flip, step_z):
    core = scal_ref[1]
    time_off = {"own": 1, "on": 2 - 2 * core, "off": 2 * core}[phase_kind]
    depth_off = jnp.where(scal_ref[0] == 1, 2 - step_z, step_z) if flip else step_z
    return 9 * time_off + 3 * depth_off


def shift_rows(value, step):
    rows = value.shape[0]
    turned = pltpu.roll(value, step % rows, 0)
    place = lax.broadcasted_iota(jnp.int32, value.shape, 0)
    return jnp.where(place == (0 if step > 0 else rows - 1), 0.0, turned)


def two_columns(weight):
    zero = jnp.zeros_like(weight)
    return jnp.concatenate(
        [jnp.concatenate([weight, zero], axis=1), jnp.concatenate([zero, weight], axis=1)], axis=0
    ).astype(BF16)


def fill_band(scal_ref, weight_ref, band, entries, outs, flip, back):
    width = LANES * len(outs)
    for i, (kind, place) in enumerate(entries):
        for j, out_place in enumerate(outs):
            step_z = place - out_place + 1
            for dy in range(3):
                lanes = slice(dy * width + j * LANES, dy * width + (j + 1) * LANES)
                if 0 <= step_z <= 2:
                    tap = tap_group(scal_ref, kind, flip, step_z) + dy
                    weight = weight_ref[weight_ref.shape[0] - 1 - tap if back else tap].astype(F32)
                    block = two_columns(weight.T if back else weight)
                else:
                    block = jnp.zeros((LANES, LANES), BF16)
                band[i * LANES : (i + 1) * LANES, lanes] = block


def place_of(scal_ref, j, depth_len, flip):
    return jnp.where(scal_ref[0] == 1, depth_len - 1 - j, j) if flip else j


def conv_columns(refs, band, lanes):
    stacked = jnp.concatenate([ref[:, lanes] for ref in refs], axis=1)
    taps = jnp.dot(stacked, band[...], preferred_element_type=F32)
    width = taps.shape[1] // 3
    return (
        shift_rows(taps[:, :width], 1)
        + taps[:, width : 2 * width]
        + shift_rows(taps[:, 2 * width :], -1)
    )


def conv_main_body(entries, flip, back, scal_ref, weight_ref, *refs):
    inputs, out_ref, band = refs[:-2], refs[-2], refs[-1]
    depth_len = out_ref.shape[0]
    fill_band(scal_ref, weight_ref, band, entries, tuple(range(depth_len)), flip, back)
    for start in range(0, out_ref.shape[2], LANES):
        lanes = slice(start, start + LANES)
        result = conv_columns(inputs, band, lanes)
        for j in range(depth_len):
            out_ref[j, :, lanes] = result[:, j * LANES : (j + 1) * LANES]


def corner_plans(groups, flip, back, scal_ref, weight_ref, inputs, bands):
    plans = {}
    for (entries, out_place), band in zip(groups, bands):
        fill_band(scal_ref, weight_ref, band, entries, (out_place,), flip, back)
        plans[out_place] = (inputs[: len(entries)], band)
        inputs = inputs[len(entries) :]
    return plans


def grad_act_body(groups, flip, scal_ref, acc_ref, image_ref, spread_ref, weight_ref, *refs):
    depth_len = acc_ref.shape[0]
    inputs, refs = refs[: 2 * len(groups)], refs[2 * len(groups) :]
    outs, bands = refs[:depth_len], refs[depth_len:]
    plans = corner_plans(groups, flip, False, scal_ref, weight_ref, inputs, bands)
    row_len = image_ref.shape[3]
    for j in range(depth_len):
        place = place_of(scal_ref, j, depth_len, flip)
        image = image_ref[place].reshape(-1, row_len)
        first, low = split(image)
        middle, last = split(image - first.astype(F32))
        stacked = jnp.concatenate([first, middle, last], axis=0)
        for start in range(0, acc_ref.shape[2], LANES):
            lanes = slice(start, start + LANES)
            grad_silu = lax.dot_general(
                stacked, spread_ref[:, lanes], (((0,), (0,)), ((), ())), preferred_element_type=F32
            )
            act = acc_ref[j, :, lanes]
            if j in plans:
                act = act + conv_columns(*plans[j], lanes)
            gate = 0.5 * jnp.tanh(0.5 * act) + 0.5
            outs[j][:, lanes] = (grad_silu * (gate * (1.0 + act * (1.0 - gate)))).astype(BF16)


def grad_feature_body(groups, flip, scal_ref, acc_ref, weight_ref, *refs):
    inputs, out_ref, bands = refs[: 2 * len(groups)], refs[2 * len(groups)], refs[2 * len(groups) + 1 :]
    plans = corner_plans(groups, flip, True, scal_ref, weight_ref, inputs, bands)
    depth_len = acc_ref.shape[0]
    for j in range(depth_len):
        place = jnp.where(scal_ref[0] == 1, depth_len - 1 - j, j) if flip else j
        for start in range(0, acc_ref.shape[2], LANES):
            lanes = slice(start, start + LANES)
            total = acc_ref[j, :, lanes]
            if j in plans:
                total = total + conv_columns(*plans[j], lanes)
            out_ref[place, :, lanes] = total.astype(BF16)


def stack_body(*refs):
    inputs, out_ref = refs[:-1], refs[-1]
    rows, packed_len = inputs[0].shape
    for i, start in enumerate(range(0, packed_len, 2 * LANES)):
        for k, ref in enumerate(inputs):
            pair = jnp.concatenate([ref[:, start : start + LANES], ref[:, start + LANES : start + 2 * LANES]], axis=0)
            value = pair.astype(F32).T
            out_ref[k * LANES : (k + 1) * LANES, 2 * rows * i : 2 * rows * (i + 1)] = value.astype(BF16)


def reach(place, outs):
    return [j for j, out_place in enumerate(outs) if 0 <= place - out_place + 1 <= 2]


def grad_weight_body(groups, outs, flip, scal_ref, *refs):
    n_out = len(outs)
    keep_ref, send_ref, right, packed = refs[-4:]
    stacks, grads = refs[: -4 - n_out], refs[-4 - n_out : -4]
    rows, packed_len = grads[0].shape
    half = LANES // 2
    width = 3 * LANES
    for i, start in enumerate(range(0, packed_len, LANES)):
        lanes = slice(start, start + LANES)
        span = slice(i * rows, (i + 1) * rows)
        for j, ref in enumerate(grads):
            value = ref[:, lanes].astype(F32)
            at = j * width
            right[span, at : at + LANES] = shift_rows(value, -1).astype(BF16)
            right[span, at + LANES : at + 2 * LANES] = ref[:, lanes]
            right[span, at + 2 * LANES : at + 3 * LANES] = shift_rows(value, 1).astype(BF16)
    entries, rows_of = [], []
    for stack, group in zip(stacks, groups):
        near = reach(group[0][1], outs)
        part = jnp.dot(
            stack[...], right[:, near[0] * width : (near[-1] + 1) * width], preferred_element_type=F32
        )
        for k, entry in enumerate(group):
            entries.append(entry)
            rows_of.append({
                j: part[k * LANES : (k + 1) * LANES, (j - near[0]) * width : (j - near[0] + 1) * width] for j in near
            })
    quarter = half // 2
    lane = lax.broadcasted_iota(jnp.int32, (quarter, LANES), 1)
    packed[27 * quarter :] = jnp.zeros((packed.shape[0] - 27 * quarter, LANES), F32)
    for kind in ("own", "on", "off"):
        for step_z in range(3):
            for dy in range(3):
                total = None
                for k, (this, place) in enumerate(entries):
                    for j, out_place in enumerate(outs):
                        if this == kind and place - out_place + 1 == step_z:
                            block = rows_of[k][j][:, dy * LANES : (dy + 1) * LANES]
                            total = block if total is None else total + block
                direct = jnp.where(lane < half, total[:quarter], total[3 * quarter :])
                turned = jnp.where(lane < half, total[quarter : 2 * quarter], total[2 * quarter : 3 * quarter])
                tap = tap_group(scal_ref, kind, flip, step_z) + dy
                packed[pl.ds(pl.multiple_of(tap * quarter, quarter), quarter), :] = direct + pltpu.roll(turned, half, 1)
    share = packed.shape[0] // 2
    core = scal_ref[1]
    keep_ref[...] = packed[pl.ds(pl.multiple_of(core * share, quarter), share), :]
    send_ref[...] = packed[pl.ds(pl.multiple_of((1 - core) * share, quarter), share), :]


def unpack_body(where_ref, *refs):
    pieces, out_ref, packed = refs[:-2], refs[-2], refs[-1]
    share = pieces[0].shape[0]
    for i, ref in enumerate(pieces):
        packed[where_ref[i]] = ref[...].astype(F32)
    flat = packed[...].reshape(-1, LANES)
    taps, height, _ = out_ref.shape
    quarter = height // 2
    for tap in range(taps):
        block = flat[tap * quarter : (tap + 1) * quarter]
        out_ref[tap, :quarter, :] = block[:, : LANES // 2]
        out_ref[tap, quarter:, :] = pltpu.roll(block, LANES // 2, 1)[:, : LANES // 2]


def pair_on(size):
    return [(i, i ^ 1) for i in range(size)]


def pair_off(size):
    return [(i, (i - 1) % size if i % 2 == 0 else (i + 1) % size) for i in range(size)]


def fold_body(pick_ref, keep_ref, got_ref, own_ref, send_ref):
    rows = own_ref.shape[0]
    for spot, out_ref in ((pick_ref[0], own_ref), (1 - pick_ref[0], send_ref)):
        span = pl.ds(pl.multiple_of(spot * rows, rows), rows)
        out_ref[...] = keep_ref[span, :] + got_ref[span, :]


def round_body(value_ref, got_ref, out_ref):
    out_ref[...] = (value_ref[...] + got_ref[...]).astype(out_ref.dtype)


def exchanges(axis, stride, size, total):
    return [(axis, [(i, i ^ (stride * bit)) for i in range(total)]) for bit in (1 << k for k in range(size.bit_length() - 1))]


def sum_over_mesh(keep, send, phases, slabs, after_finish):
    phase = lax.axis_index("phase")
    core, column = phase % 2, phase // 2 % 2
    part_shape = (keep.shape[0] // 2, LANES)
    across = [(p, p ^ 2) for p in range(phases)]
    part, other = call(
        "fold",
        fold_body,
        [jax.ShapeDtypeStruct(part_shape, F32)] * 2,
        (column.reshape(1), keep, lax.ppermute(send, "phase", pair_on(phases))),
        "SVV",
        nbytes=100000,
    )
    part = part + lax.ppermute(other, "phase", across)
    steps = exchanges("slab", 1, slabs, slabs) + exchanges("phase", 4, phases // 4, phases)
    for axis, perm in steps[:-1]:
        part = part + lax.ppermute(part, axis, perm)
    axis, perm = steps[-1]
    part = call(
        "finish",
        round_body,
        jax.ShapeDtypeStruct(part_shape, BF16),
        (part, lax.ppermute(part, axis, perm)),
        "VV",
        nbytes=30000,
        after=after_finish,
    )
    pieces = [part, lax.ppermute(part, "phase", across)]
    pieces += [lax.ppermute(piece, "phase", pair_on(phases)) for piece in pieces]
    spots = [2 * core + column, 2 * core + 1 - column]
    spots += [2 * (1 - core) + column, 2 * (1 - core) + 1 - column]
    return pieces, jnp.stack(spots).astype(jnp.int32)


def local(phases, slabs, features, conv_weight, projection, grad_out, sens, mask):
    _, depth_len, row_len, packed_len = features.shape
    channels = conv_weight.shape[1]
    col_len = packed_len // channels
    coils = sens.shape[1]
    taps = conv_weight.shape[0]
    slab, core = lax.axis_index("slab"), lax.axis_index("phase") % 2
    flip = slabs == 2
    scal = jnp.stack([slab, core]).astype(jnp.int32)
    on, off = pair_on(phases), pair_off(phases)

    def pass_phase(value, perm):
        return lax.ppermute(value, "phase", perm)

    if flip:
        order = list(range(depth_len))
        edges = [(depth_len - 1, depth_len, [(0, 1), (1, 0)])]
        pick = lambda j: jnp.where(slab == 1, depth_len - 1 - j, j)
    else:
        order = list(range(depth_len))
        up = [(i, i + 1) for i in range(slabs - 1)]
        edges = [(depth_len - 1, -1, up), (0, depth_len, [(j, i) for i, j in up])]
        pick = lambda j: j

    first_sent = [edge[0] for edge in edges]

    def halo(own):
        off_in = {}
        for j in first_sent + [j for j in order if j not in first_sent]:
            off_in[j] = pass_phase(own[j], off)
        slab_in = [lax.ppermute(own[edge[0]], "slab", edge[2]) for edge in edges]
        on_in = [pass_phase(own[j], on) for j in order]
        corner_off = [lax.ppermute(off_in[edge[0]], "slab", edge[2]) for edge in edges]
        corner_on = [pass_phase(value, on) for value in slab_in]
        corners = []
        for a, b in zip(corner_off, corner_on):
            corners += [a, b]
        full = list(own) + on_in + [off_in[j] for j in order]
        ends = [list(values) for values in zip(slab_in, corner_off, corner_on)]
        return full, full + slab_in, corners, ends

    main_entries = (
        [(kind, j) for kind in ("own", "on", "off") for j in order] + [("own", edge[1]) for edge in edges]
    )
    corner_entries = []
    corner_groups = []
    for edge in edges:
        near = min(max(edge[1], 0), depth_len - 1)
        corner_groups.append(([("off", edge[1]), ("on", edge[1])], near))
        corner_entries += [("off", edge[1]), ("on", edge[1])]
    corner_groups.sort(key=lambda g: g[1])

    high, low = dft_packed(row_len)
    high, low = jnp.asarray(high), jnp.asarray(low)
    lines = depth_len * coils * col_len
    grad_now = grad_out[0]
    line_shape = (lines, 2 * row_len)
    slice_shape = (row_len, packed_len)
    slab_shape = (depth_len, row_len, packed_len)
    scratch = [pltpu.VMEM(line_shape, BF16)] * 2
    coil_flops = 3 * 2 * lines * (2 * row_len) ** 2
    own_lines, sent_lines = call(
        "coil_forward",
        coil_forward_body,
        [jax.ShapeDtypeStruct(line_shape, F32), jax.ShapeDtypeStruct(line_shape, BF16)],
        (grad_now, sens, high, low),
        "VVVV",
        scratch=scratch,
        flops=coil_flops,
        nbytes=4000000,
    )
    own_slices = [lax.dynamic_index_in_dim(features[0], pick(j), 0, keepdims=False) for j in order]
    full_in, main_in, corner_in, ends_in = halo(own_slices)
    other_lines = [
        lax.ppermute(sent_lines, "slab", [(i, (i + k) % slabs) for i in range(slabs)]) for k in range(1, slabs)
    ]
    spread = -(projection[:, None, None, :] * jnp.eye(col_len, dtype=BF16)[None, :, :, None])
    spread = spread.reshape(2 * col_len, packed_len)
    spread = jnp.concatenate([spread] * 3, axis=0)

    bands = [pltpu.VMEM((len(g[0]) * LANES, 3 * LANES), BF16) for g in corner_groups]

    conv_flops = 2 * row_len * len(main_entries) * packed_len * 3 * depth_len * LANES
    small_flops = 2 * row_len * 2 * packed_len * 3 * LANES

    def conv_main(name, back, inputs, after=()):
        return call(
            name,
            functools.partial(conv_main_body, main_entries, flip, back),
            jax.ShapeDtypeStruct(slab_shape, F32),
            (scal, conv_weight, *inputs),
            "SV" + "V" * len(inputs),
            scratch=[pltpu.VMEM((len(main_entries) * LANES, 3 * depth_len * LANES), BF16)],
            flops=conv_flops,
            nbytes=5000000,
            after=after,
        )

    def stack(name, inputs):
        return call(
            name,
            stack_body,
            pltpu.VMEM((len(inputs) * LANES, packed_len // LANES * row_len), BF16),
            tuple(inputs),
            "V" * len(inputs),
            nbytes=5000000,
        )

    acc = conv_main("conv_act", False, main_in)
    grad_image = call(
        "coil_back",
        functools.partial(coil_backward_body, slabs),
        jax.ShapeDtypeStruct(grad_now.shape, F32),
        (grad_now, sens, mask[0], high, low, own_lines, *other_lines),
        "VVVVVV" + "V" * len(other_lines),
        after=[acc],
        scratch=scratch,
        flops=coil_flops,
        nbytes=5000000,
    )

    stack_full = stack("stack_full", full_in)
    grad_act = call(
        "grad_act",
        functools.partial(grad_act_body, corner_groups, flip),
        [pltpu.VMEM(slice_shape, BF16)] * depth_len,
        (scal, acc, grad_image, spread, conv_weight, *corner_in),
        "SVVVV" + "V" * len(corner_in),
        flops=small_flops,
        nbytes=4000000,
        scratch=bands,
        after=[stack_full],
    )

    _, main_grad, corner_grad, _ = halo(grad_act)

    share = (taps + 1) // 2 * channels // 2
    stacks = [stack_full] + [stack("stack_end", values) for values in ends_in]
    weight_groups = [[(kind, j) for kind in ("own", "on", "off") for j in order]]
    weight_groups += [[(kind, edge[1]) for kind in ("own", "off", "on")] for edge in edges]
    keep, send = call(
        "grad_weight",
        functools.partial(grad_weight_body, weight_groups, tuple(order), flip),
        [jax.ShapeDtypeStruct((share, LANES), F32)] * 2,
        (scal, *stacks, *grad_act),
        "S" + "M" * (len(stacks) + depth_len),
        after=[],
        scratch=[
            pltpu.VMEM((packed_len // LANES * row_len, 3 * depth_len * LANES), BF16),
            pltpu.VMEM((2 * share, LANES), F32),
        ],
        flops=conv_flops,
        nbytes=5000000,
    )

    acc_back = conv_main("conv_back", True, main_grad)
    pieces, spots = sum_over_mesh(keep, send, phases, slabs, [acc_back])
    grad_weight = call(
        "unpack",
        unpack_body,
        jax.ShapeDtypeStruct(conv_weight.shape, F32),
        (spots, *pieces),
        "S" + "V" * len(pieces),
        scratch=[pltpu.VMEM((len(pieces),) + pieces[0].shape, F32)],
        nbytes=1000000,
    )
    grad_features = call(
        "grad_features",
        functools.partial(grad_feature_body, corner_groups, flip),
        jax.ShapeDtypeStruct(slab_shape, BF16),
        (scal, acc_back, conv_weight, *corner_grad),
        "SVV" + "V" * len(corner_grad),
        scratch=bands,
        flops=small_flops,
        nbytes=4000000,
    )

    return (grad_image[None], grad_features[None], grad_weight)


def solution(mesh):
    in_specs = (
        P("phase", "slab", None, None),
        P(),
        P(),
        P("phase", "slab", None, None, None),
        P("slab", None, None, None, None),
        P("phase", None, None),
    )
    out_specs = (P("phase", "slab", None, None, None), P("phase", "slab", None, None), P())
    body = functools.partial(local, mesh.shape["phase"], mesh.shape["slab"])
    return jax.shard_map(body, mesh=mesh, in_specs=in_specs, out_specs=out_specs, check_vma=False)
```

```python
import functools
import math

import jax
import jax.numpy as jnp
import ml_dtypes
import numpy as np
from jax import lax
from jax.experimental import pallas as pl
from jax.experimental.pallas import tpu as pltpu
from jax.sharding import PartitionSpec as P

F32, BF16 = jnp.float32, jnp.bfloat16
VMEM = pl.BlockSpec(memory_space=pltpu.VMEM)
SMEM = pl.BlockSpec(memory_space=pltpu.SMEM)
LIMIT = 48 * 1024 * 1024
LANES = 128


ANY = pl.BlockSpec(memory_space=pl.ANY)
SPECS = {"S": SMEM, "V": VMEM, "M": VMEM, "H": VMEM}


def call(name, body, outs, ins, kinds, scratch=(), flops=0, nbytes=0, after=()):
    count, waits = len(ins), len(after)

    def run(*refs):
        body(*refs[:count], *refs[count + waits :])

    spaces = {"M": pltpu.VMEM, "H": pltpu.HBM}
    ins = [
        pltpu.with_memory_space_constraint(x, spaces[kind]) if kind in spaces else x for x, kind in zip(ins, kinds)
    ]
    return pl.pallas_call(
        run,
        out_shape=outs,
        in_specs=[SPECS[kind] for kind in kinds] + [ANY] * waits,
        out_specs=[VMEM] * len(outs) if isinstance(outs, (list, tuple)) else VMEM,
        scratch_shapes=list(scratch),
        compiler_params=pltpu.CompilerParams(vmem_limit_bytes=LIMIT),
        cost_estimate=pl.CostEstimate(flops=flops, bytes_accessed=nbytes, transcendentals=0),
        name=name,
    )(*ins, *after)


def dft_packed(length):
    full = length // LANES * LANES
    part = np.concatenate([np.zeros(full), np.ones(full), np.zeros(length - full), np.ones(length - full)])
    index = np.concatenate([np.arange(full)] * 2 + [np.arange(full, length)] * 2)
    angle = (index[:, None] * index[None, :] % length) * (2.0 * math.pi / length)
    cosine, sine = np.cos(angle), np.sin(angle)
    same = part[:, None] == part[None, :]
    matrix = np.where(same, cosine, np.where(part[:, None] == 0, -sine, sine)) / math.sqrt(length)
    high = matrix.astype(ml_dtypes.bfloat16)
    low = (matrix - high.astype(np.float64)).astype(ml_dtypes.bfloat16)
    return high, low


def split(value):
    high = value.astype(BF16)
    return high, (value - high.astype(F32)).astype(BF16)


def dot3(high, low, mat_high, mat_low, dims):
    dot = functools.partial(lax.dot_general, dimension_numbers=(dims, ((), ())), preferred_element_type=F32)
    return dot(high, mat_high) + (dot(high, mat_low) + dot(low, mat_high))


def coil_forward_body(grad_ref, sens_ref, high_ref, low_ref, out_ref, send_ref, x_high, x_low):
    depth_len, coils, _, col_len, row_len = sens_ref.shape
    full = row_len // LANES * LANES
    count = coils * col_len
    for z in range(depth_len):
        sens_r, sens_i = sens_ref[z, :, 0], sens_ref[z, :, 1]
        img_r, img_i = grad_ref[z, 0][None], grad_ref[z, 1][None]
        real = sens_r * img_r - sens_i * img_i
        imag = sens_r * img_i + sens_i * img_r
        rest = jnp.concatenate([real[..., full:], imag[..., full:]], axis=-1)
        for piece, start in ((real[..., :full], 0), (imag[..., :full], full), (rest, 2 * full)):
            width = piece.shape[-1]
            high, low = split(piece.reshape(count, width))
            x_high[z * count : (z + 1) * count, start : start + width] = high
            x_low[z * count : (z + 1) * count, start : start + width] = low
    result = dot3(x_high[...], x_low[...], high_ref[...], low_ref[...], ((1,), (0,)))
    out_ref[...] = result
    send_ref[...] = result.astype(BF16)


def coil_backward_body(slabs, grad_ref, sens_ref, mask_ref, high_ref, low_ref, own_ref, *refs):
    others, out_ref, x_high, x_low = refs[: slabs - 1], refs[-3], refs[-2], refs[-1]
    depth_len, coils, _, col_len, row_len = sens_ref.shape
    total = slabs * depth_len
    full = row_len // LANES * LANES
    rem = row_len - full
    count = coils * col_len
    mask = mask_ref[...].astype(F32)

    def table(turn):
        real = jnp.zeros((1, row_len), F32)
        imag = jnp.zeros((1, row_len), F32)
        has_imag = False
        for kz in range(total):
            angle = 2.0 * math.pi * ((kz * turn) % total) / total
            cosine, sine = round(math.cos(angle), 15) / total, round(math.sin(angle), 15) / total
            real = real + mask[kz : kz + 1] * cosine
            if sine != 0.0:
                imag = imag + mask[kz : kz + 1] * sine
                has_imag = True
        real_rest = jnp.concatenate([real[:, full:], real[:, full:]], axis=-1)
        imag_rest = jnp.concatenate([-imag[:, full:], imag[:, full:]], axis=-1)
        return real[:, :full], imag[:, :full], real_rest, imag_rest, has_imag

    tables = {}
    for z in range(depth_len):
        sums = None
        for step in range(slabs):
            src = own_ref if step == 0 else others[step - 1]
            for zin in range(depth_len):
                turn = (step * depth_len + z - zin) % total
                if turn not in tables:
                    tables[turn] = table(turn)
                real, imag, real_rest, imag_rest, has_imag = tables[turn]
                block = src[zin * count : (zin + 1) * count, :].astype(F32)
                v_r, v_i, v_rest = block[:, :full], block[:, full : 2 * full], block[:, 2 * full :]
                if has_imag:
                    terms = (
                        real * v_r - imag * v_i,
                        real * v_i + imag * v_r,
                        real_rest * v_rest + imag_rest * pltpu.roll(v_rest, rem, 1),
                    )
                else:
                    terms = (real * v_r, real * v_i, real_rest * v_rest)
                sums = terms if sums is None else tuple(a + b for a, b in zip(sums, terms))
        for piece, start in zip(sums, (0, full, 2 * full)):
            high, low = split(piece)
            x_high[z * count : (z + 1) * count, start : start + piece.shape[1]] = high
            x_low[z * count : (z + 1) * count, start : start + piece.shape[1]] = low
    back = dot3(x_high[...], x_low[...], high_ref[...], low_ref[...], ((1,), (1,)))
    for z in range(depth_len):
        sens_r, sens_i = sens_ref[z, :, 0], sens_ref[z, :, 1]
        block = back[z * count : (z + 1) * count].reshape(coils, col_len, 2 * row_len)
        b_r, b_i, b_rest = block[..., :full], block[..., full : 2 * full], block[..., 2 * full :]
        s_r, s_i = sens_r[..., :full], sens_i[..., :full]
        out_ref[z, 0, :, :full] = grad_ref[z, 0, :, :full] - jnp.sum(s_r * b_r + s_i * b_i, axis=0)
        out_ref[z, 1, :, :full] = grad_ref[z, 1, :, :full] - jnp.sum(s_r * b_i - s_i * b_r, axis=0)
        s_rest = jnp.concatenate([sens_r[..., full:], sens_i[..., full:]], axis=-1)
        turned = pltpu.roll(b_rest, rem, 2)
        along = jnp.sum(s_rest * b_rest, axis=0)
        across = jnp.sum(s_rest * turned, axis=0)
        real = along + pltpu.roll(along, rem, 1)
        imag = across - pltpu.roll(across, rem, 1)
        out_ref[z, 0, :, full:] = grad_ref[z, 0, :, full:] - real[:, :rem]
        out_ref[z, 1, :, full:] = grad_ref[z, 1, :, full:] - imag[:, :rem]


def tap_group(scal_ref, phase_kind, flip, step_z):
    core = scal_ref[1]
    time_off = {"own": 1, "on": 2 - 2 * core, "off": 2 * core}[phase_kind]
    depth_off = jnp.where(scal_ref[0] == 1, 2 - step_z, step_z) if flip else step_z
    return 9 * time_off + 3 * depth_off


def shift_rows(value, step):
    rows = value.shape[0]
    turned = pltpu.roll(value, step % rows, 0)
    place = lax.broadcasted_iota(jnp.int32, value.shape, 0)
    return jnp.where(place == (0 if step > 0 else rows - 1), 0.0, turned)


def two_columns(weight):
    zero = jnp.zeros_like(weight)
    return jnp.concatenate(
        [jnp.concatenate([weight, zero], axis=1), jnp.concatenate([zero, weight], axis=1)], axis=0
    ).astype(BF16)


def fill_band(scal_ref, weight_ref, band, entries, outs, flip, back):
    width = LANES * len(outs)
    made = {}
    for i, (kind, place) in enumerate(entries):
        for j, out_place in enumerate(outs):
            step_z = place - out_place + 1
            for dy in range(3):
                lanes = slice(dy * width + j * LANES, dy * width + (j + 1) * LANES)
                if 0 <= step_z <= 2:
                    if (kind, step_z, dy) not in made:
                        tap = tap_group(scal_ref, kind, flip, step_z) + dy
                        weight = weight_ref[weight_ref.shape[0] - 1 - tap if back else tap].astype(F32)
                        made[kind, step_z, dy] = two_columns(weight.T if back else weight)
                    block = made[kind, step_z, dy]
                else:
                    block = jnp.zeros((LANES, LANES), BF16)
                band[i * LANES : (i + 1) * LANES, lanes] = block


def place_of(scal_ref, j, depth_len, flip):
    return jnp.where(scal_ref[0] == 1, depth_len - 1 - j, j) if flip else j


def conv_columns(refs, band, lanes):
    stacked = jnp.concatenate([ref[:, lanes] for ref in refs], axis=1)
    taps = jnp.dot(stacked, band[...], preferred_element_type=F32)
    width = taps.shape[1] // 3
    return (
        shift_rows(taps[:, :width], 1)
        + taps[:, width : 2 * width]
        + shift_rows(taps[:, 2 * width :], -1)
    )


def conv_main_body(entries, flip, back, scal_ref, weight_ref, *refs):
    inputs, out_ref, band = refs[:-2], refs[-2], refs[-1]
    depth_len = out_ref.shape[0]
    fill_band(scal_ref, weight_ref, band, entries, tuple(range(depth_len)), flip, back)
    for start in range(0, out_ref.shape[2], LANES):
        lanes = slice(start, start + LANES)
        result = conv_columns(inputs, band, lanes)
        for j in range(depth_len):
            out_ref[j, :, lanes] = result[:, j * LANES : (j + 1) * LANES]


def corner_plans(groups, flip, back, scal_ref, weight_ref, inputs, bands):
    plans = {}
    for (entries, out_place), band in zip(groups, bands):
        fill_band(scal_ref, weight_ref, band, entries, (out_place,), flip, back)
        plans[out_place] = (inputs[: len(entries)], band)
        inputs = inputs[len(entries) :]
    return plans


def stack_body(*refs):
    inputs, out_ref = refs[:-1], refs[-1]
    rows, packed_len = inputs[0].shape
    for i, start in enumerate(range(0, packed_len, 2 * LANES)):
        for k, ref in enumerate(inputs):
            pair = jnp.concatenate([ref[:, start : start + LANES], ref[:, start + LANES : start + 2 * LANES]], axis=0)
            value = pair.astype(F32).T
            out_ref[k * LANES : (k + 1) * LANES, 2 * rows * i : 2 * rows * (i + 1)] = value.astype(BF16)


def grad_act_body(groups, flip, scal_ref, acc_ref, image_ref, spread_ref, weight_ref, *refs):
    depth_len, count = acc_ref.shape[0], len(groups)
    slab_in, inputs, refs = refs[:count], refs[count : 3 * count], refs[3 * count :]
    outs, ends, bands = refs[:depth_len], refs[depth_len : depth_len + count], refs[depth_len + count :]
    for k, end in enumerate(ends):
        stack_body(slab_in[k], *inputs[2 * k : 2 * k + 2], end)
    plans = corner_plans(groups, flip, False, scal_ref, weight_ref, inputs, bands)
    row_len = image_ref.shape[3]
    for j in range(depth_len):
        place = place_of(scal_ref, j, depth_len, flip)
        image = image_ref[place].reshape(-1, row_len)
        first, low = split(image)
        middle, last = split(image - first.astype(F32))
        stacked = jnp.concatenate([first, middle, last], axis=0)
        for start in range(0, acc_ref.shape[2], LANES):
            lanes = slice(start, start + LANES)
            grad_silu = lax.dot_general(
                stacked, spread_ref[:, lanes], (((0,), (0,)), ((), ())), preferred_element_type=F32
            )
            act = acc_ref[j, :, lanes]
            if j in plans:
                act = act + conv_columns(*plans[j], lanes)
            gate = 0.5 * jnp.tanh(0.5 * act) + 0.5
            outs[j][:, lanes] = (grad_silu * (gate * (1.0 + act * (1.0 - gate)))).astype(BF16)


def grad_feature_body(groups, flip, scal_ref, acc_ref, weight_ref, *refs):
    inputs, out_ref, bands = refs[: 2 * len(groups)], refs[2 * len(groups)], refs[2 * len(groups) + 1 :]
    plans = corner_plans(groups, flip, True, scal_ref, weight_ref, inputs, bands)
    depth_len = acc_ref.shape[0]
    for j in range(depth_len):
        place = jnp.where(scal_ref[0] == 1, depth_len - 1 - j, j) if flip else j
        for start in range(0, acc_ref.shape[2], LANES):
            lanes = slice(start, start + LANES)
            total = acc_ref[j, :, lanes]
            if j in plans:
                total = total + conv_columns(*plans[j], lanes)
            out_ref[place, :, lanes] = total.astype(BF16)


def reach(place, outs):
    return [j for j, out_place in enumerate(outs) if 0 <= place - out_place + 1 <= 2]


def grad_weight_body(groups, outs, flip, scal_ref, *refs):
    n_out = len(outs)
    keep_ref, send_ref, right, packed = refs[-4:]
    stacks, grads = refs[: -4 - n_out], refs[-4 - n_out : -4]
    rows, packed_len = grads[0].shape
    half = LANES // 2
    width = 3 * LANES
    for i, start in enumerate(range(0, packed_len, LANES)):
        lanes = slice(start, start + LANES)
        span = slice(i * rows, (i + 1) * rows)
        for j, ref in enumerate(grads):
            value = ref[:, lanes].astype(F32)
            at = j * width
            right[span, at : at + LANES] = shift_rows(value, -1).astype(BF16)
            right[span, at + LANES : at + 2 * LANES] = ref[:, lanes]
            right[span, at + 2 * LANES : at + 3 * LANES] = shift_rows(value, 1).astype(BF16)
    entries, rows_of = [], []
    for stack, group in zip(stacks, groups):
        near = reach(group[0][1], outs)
        part = jnp.dot(
            stack[...], right[:, near[0] * width : (near[-1] + 1) * width], preferred_element_type=F32
        )
        for k, entry in enumerate(group):
            entries.append(entry)
            rows_of.append({
                j: part[k * LANES : (k + 1) * LANES, (j - near[0]) * width : (j - near[0] + 1) * width] for j in near
            })
    quarter = half // 2
    lane = lax.broadcasted_iota(jnp.int32, (quarter, LANES), 1)
    packed[27 * quarter :] = jnp.zeros((packed.shape[0] - 27 * quarter, LANES), F32)
    for kind in ("own", "on", "off"):
        for step_z in range(3):
            for dy in range(3):
                total = None
                for k, (this, place) in enumerate(entries):
                    for j, out_place in enumerate(outs):
                        if this == kind and place - out_place + 1 == step_z:
                            block = rows_of[k][j][:, dy * LANES : (dy + 1) * LANES]
                            total = block if total is None else total + block
                direct = jnp.where(lane < half, total[:quarter], total[3 * quarter :])
                turned = jnp.where(lane < half, total[quarter : 2 * quarter], total[2 * quarter : 3 * quarter])
                tap = tap_group(scal_ref, kind, flip, step_z) + dy
                packed[pl.ds(pl.multiple_of(tap * quarter, quarter), quarter), :] = direct + pltpu.roll(turned, half, 1)
    share = packed.shape[0] // 2
    core = scal_ref[1]
    keep_ref[...] = packed[pl.ds(pl.multiple_of(core * share, quarter), share), :]
    send_ref[...] = packed[pl.ds(pl.multiple_of((1 - core) * share, quarter), share), :]


def unpack_body(where_ref, *refs):
    pieces, out_ref, packed = refs[:-2], refs[-2], refs[-1]
    share = pieces[0].shape[0]
    for i, ref in enumerate(pieces):
        packed[where_ref[i]] = ref[...].astype(F32)
    flat = packed[...].reshape(-1, LANES)
    taps, height, _ = out_ref.shape
    quarter = height // 2
    for tap in range(taps):
        block = flat[tap * quarter : (tap + 1) * quarter]
        out_ref[tap, :quarter, :] = block[:, : LANES // 2]
        out_ref[tap, quarter:, :] = pltpu.roll(block, LANES // 2, 1)[:, : LANES // 2]


def final_body(groups, flip, scal_ref, acc_ref, weight_ref, *refs):
    corners, count = refs[: 2 * len(groups)], 2 * len(groups)
    where_ref, pieces = refs[count], refs[count + 1 : count + 5]
    features_ref, taps_ref, packed, bands = refs[count + 5], refs[count + 6], refs[-1], refs[count + 7 : -1]
    unpack_body(where_ref, *pieces, taps_ref, packed)
    grad_feature_body(groups, flip, scal_ref, acc_ref, weight_ref, *corners, features_ref, *bands)


def pair_on(size):
    return [(i, i ^ 1) for i in range(size)]


def pair_off(size):
    return [(i, (i - 1) % size if i % 2 == 0 else (i + 1) % size) for i in range(size)]


def fold_body(pick_ref, keep_ref, got_ref, own_ref, send_ref):
    rows = own_ref.shape[0]
    for spot, out_ref in ((pick_ref[0], own_ref), (1 - pick_ref[0], send_ref)):
        span = pl.ds(pl.multiple_of(spot * rows, rows), rows)
        out_ref[...] = keep_ref[span, :] + got_ref[span, :]


def round_body(value_ref, got_ref, out_ref):
    out_ref[...] = (value_ref[...] + got_ref[...]).astype(out_ref.dtype)


def exchanges(axis, stride, size, total):
    return [(axis, [(i, i ^ (stride * bit)) for i in range(total)]) for bit in (1 << k for k in range(size.bit_length() - 1))]


def sum_over_mesh(keep, send, phases, slabs, after_finish):
    phase = lax.axis_index("phase")
    core, column = phase % 2, phase // 2 % 2
    part_shape = (keep.shape[0] // 2, LANES)
    across = [(p, p ^ 2) for p in range(phases)]
    part, other = call(
        "fold",
        fold_body,
        [jax.ShapeDtypeStruct(part_shape, F32)] * 2,
        (column.reshape(1), keep, lax.ppermute(send, "phase", pair_on(phases))),
        "SVV",
        nbytes=100000,
    )
    part = part + lax.ppermute(other, "phase", across)
    steps = exchanges("slab", 1, slabs, slabs) + exchanges("phase", 4, phases // 4, phases)
    for axis, perm in steps[:-1]:
        part = part + lax.ppermute(part, axis, perm)
    axis, perm = steps[-1]
    part = call(
        "finish",
        round_body,
        jax.ShapeDtypeStruct(part_shape, BF16),
        (part, lax.ppermute(part, axis, perm)),
        "VV",
        nbytes=30000,
        after=after_finish,
    )
    pieces = [part, lax.ppermute(part, "phase", across)]
    pieces += [lax.ppermute(piece, "phase", pair_on(phases)) for piece in pieces]
    spots = [2 * core + column, 2 * core + 1 - column]
    spots += [2 * (1 - core) + column, 2 * (1 - core) + 1 - column]
    return pieces, jnp.stack(spots).astype(jnp.int32)


def local(phases, slabs, features, conv_weight, projection, grad_out, sens, mask):
    _, depth_len, row_len, packed_len = features.shape
    channels = conv_weight.shape[1]
    col_len = packed_len // channels
    coils = sens.shape[1]
    taps = conv_weight.shape[0]
    slab, core = lax.axis_index("slab"), lax.axis_index("phase") % 2
    flip = slabs == 2
    scal = jnp.stack([slab, core]).astype(jnp.int32)
    on, off = pair_on(phases), pair_off(phases)

    def pass_phase(value, perm):
        return lax.ppermute(value, "phase", perm)

    if flip:
        order = list(range(depth_len))
        edges = [(depth_len - 1, depth_len, [(0, 1), (1, 0)])]
        pick = lambda j: jnp.where(slab == 1, depth_len - 1 - j, j)
    else:
        order = list(range(depth_len))
        up = [(i, i + 1) for i in range(slabs - 1)]
        edges = [(depth_len - 1, -1, up), (0, depth_len, [(j, i) for i, j in up])]
        pick = lambda j: j

    first_sent = [edge[0] for edge in edges]

    def halo(own):
        off_in = {}
        for j in first_sent + [j for j in order if j not in first_sent]:
            off_in[j] = pass_phase(own[j], off)
        slab_in = [lax.ppermute(own[edge[0]], "slab", edge[2]) for edge in edges]
        on_in = [pass_phase(own[j], on) for j in order]
        corner_off = [lax.ppermute(off_in[edge[0]], "slab", edge[2]) for edge in edges]
        corner_on = [pass_phase(value, on) for value in slab_in]
        corners = []
        for a, b in zip(corner_off, corner_on):
            corners += [a, b]
        full = list(own) + on_in + [off_in[j] for j in order]
        ends = [list(values) for values in zip(slab_in, corner_off, corner_on)]
        return full, full + slab_in, corners, ends

    main_entries = (
        [(kind, j) for kind in ("own", "on", "off") for j in order] + [("own", edge[1]) for edge in edges]
    )
    corner_entries = []
    corner_groups = []
    for edge in edges:
        near = min(max(edge[1], 0), depth_len - 1)
        corner_groups.append(([("off", edge[1]), ("on", edge[1])], near))
        corner_entries += [("off", edge[1]), ("on", edge[1])]
    corner_groups.sort(key=lambda g: g[1])

    high, low = dft_packed(row_len)
    high, low = jnp.asarray(high), jnp.asarray(low)
    lines = depth_len * coils * col_len
    grad_now = grad_out[0]
    line_shape = (lines, 2 * row_len)
    slice_shape = (row_len, packed_len)
    slab_shape = (depth_len, row_len, packed_len)
    scratch = [pltpu.VMEM(line_shape, BF16)] * 2
    coil_flops = 3 * 2 * lines * (2 * row_len) ** 2
    own_lines, sent_lines = call(
        "coil_forward",
        coil_forward_body,
        [jax.ShapeDtypeStruct(line_shape, F32), jax.ShapeDtypeStruct(line_shape, BF16)],
        (grad_now, sens, high, low),
        "VHHH",
        scratch=scratch,
        flops=coil_flops,
        nbytes=4000000,
    )
    own_slices = [lax.dynamic_index_in_dim(features[0], pick(j), 0, keepdims=False) for j in order]
    full_in, main_in, corner_in, ends_in = halo(own_slices)
    other_lines = [
        lax.ppermute(sent_lines, "slab", [(i, (i + k) % slabs) for i in range(slabs)]) for k in range(1, slabs)
    ]
    spread = -(projection[:, None, None, :] * jnp.eye(col_len, dtype=BF16)[None, :, :, None])
    spread = spread.reshape(2 * col_len, packed_len)
    spread = jnp.concatenate([spread] * 3, axis=0)

    bands = [pltpu.VMEM((len(g[0]) * LANES, 3 * LANES), BF16) for g in corner_groups]

    conv_flops = 2 * row_len * len(main_entries) * packed_len * 3 * depth_len * LANES
    small_flops = 2 * row_len * 2 * packed_len * 3 * LANES

    def conv_main(name, back, inputs, after=()):
        return call(
            name,
            functools.partial(conv_main_body, main_entries, flip, back),
            jax.ShapeDtypeStruct(slab_shape, F32),
            (scal, conv_weight, *inputs),
            "SV" + "V" * len(inputs),
            scratch=[pltpu.VMEM((len(main_entries) * LANES, 3 * depth_len * LANES), BF16)],
            flops=conv_flops,
            nbytes=5000000,
            after=after,
        )

    def stack(name, inputs):
        return call(
            name,
            stack_body,
            jax.ShapeDtypeStruct((len(inputs) * LANES, packed_len // LANES * row_len), BF16),
            tuple(inputs),
            "V" * len(inputs),
            nbytes=5000000,
        )

    acc = conv_main("conv_act", False, main_in)
    grad_image = call(
        "coil_back",
        functools.partial(coil_backward_body, slabs),
        jax.ShapeDtypeStruct(grad_now.shape, F32),
        (grad_now, sens, mask[0], high, low, own_lines, *other_lines),
        "VVVVVV" + "V" * len(other_lines),
        after=[acc],
        scratch=scratch,
        flops=coil_flops,
        nbytes=5000000,
    )

    stack_full = stack("stack_full", full_in)
    grad_outs = call(
        "grad_act",
        functools.partial(grad_act_body, corner_groups, flip),
        [pltpu.VMEM(slice_shape, BF16)] * depth_len
        + [pltpu.VMEM((3 * LANES, packed_len // LANES * row_len), BF16)] * len(edges),
        (scal, acc, grad_image, spread, conv_weight, *[values[0] for values in ends_in], *corner_in),
        "SVHVV" + "V" * (len(edges) + len(corner_in)),
        flops=small_flops,
        nbytes=4000000,
        scratch=bands,
        after=[stack_full],
    )

    grad_act, stack_ends = grad_outs[:depth_len], grad_outs[depth_len:]
    _, main_grad, corner_grad, _ = halo(grad_act)

    share = (taps + 1) // 2 * channels // 2
    stacks = [stack_full, *stack_ends]
    weight_groups = [[(kind, j) for kind in ("own", "on", "off") for j in order]]
    weight_groups += [[(kind, edge[1]) for kind in ("own", "off", "on")] for edge in edges]
    keep, send = call(
        "grad_weight",
        functools.partial(grad_weight_body, weight_groups, tuple(order), flip),
        [jax.ShapeDtypeStruct((share, LANES), F32)] * 2,
        (scal, *stacks, *grad_act),
        "SV" + "M" * (len(stacks) - 1 + depth_len),
        after=[],
        scratch=[
            pltpu.VMEM((packed_len // LANES * row_len, 3 * depth_len * LANES), BF16),
            pltpu.VMEM((2 * share, LANES), F32),
        ],
        flops=conv_flops,
        nbytes=5000000,
    )

    acc_back = conv_main("conv_back", True, main_grad)
    pieces, spots = sum_over_mesh(keep, send, phases, slabs, [acc_back])
    grad_features, grad_weight = call(
        "finish_both",
        functools.partial(final_body, corner_groups, flip),
        [jax.ShapeDtypeStruct(slab_shape, BF16), jax.ShapeDtypeStruct(conv_weight.shape, F32)],
        (scal, acc_back, conv_weight, *corner_grad, spots, *pieces),
        "SVV" + "V" * len(corner_grad) + "S" + "V" * len(pieces),
        scratch=bands + [pltpu.VMEM((len(pieces),) + pieces[0].shape, F32)],
        flops=small_flops,
        nbytes=4000000,
    )
    return (grad_image[None], grad_features[None], grad_weight)


def solution(mesh):
    in_specs = (
        P("phase", "slab", None, None),
        P(),
        P(),
        P("phase", "slab", None, None, None),
        P("slab", None, None, None, None),
        P("phase", None, None),
    )
    out_specs = (P("phase", "slab", None, None, None), P("phase", "slab", None, None), P())
    body = functools.partial(local, mesh.shape["phase"], mesh.shape["slab"])
    return jax.shard_map(body, mesh=mesh, in_specs=in_specs, out_specs=out_specs, check_vma=False)
```

```python
import functools
import math

import jax
import jax.numpy as jnp
import ml_dtypes
import numpy as np
from jax import lax
from jax.experimental import pallas as pl
from jax.experimental.pallas import tpu as pltpu
from jax.sharding import PartitionSpec as P

F32, BF16 = jnp.float32, jnp.bfloat16
VMEM = pl.BlockSpec(memory_space=pltpu.VMEM)
SMEM = pl.BlockSpec(memory_space=pltpu.SMEM)
LIMIT = 48 * 1024 * 1024
LANES = 128


ANY = pl.BlockSpec(memory_space=pl.ANY)
SPECS = {"S": SMEM, "V": VMEM, "M": VMEM, "H": VMEM}


def call(name, body, outs, ins, kinds, scratch=(), flops=0, nbytes=0, after=()):
    count, waits = len(ins), len(after)

    def run(*refs):
        body(*refs[:count], *refs[count + waits :])

    spaces = {"M": pltpu.VMEM, "H": pltpu.HBM}
    ins = [
        pltpu.with_memory_space_constraint(x, spaces[kind]) if kind in spaces else x for x, kind in zip(ins, kinds)
    ]
    return pl.pallas_call(
        run,
        out_shape=outs,
        in_specs=[SPECS[kind] for kind in kinds] + [ANY] * waits,
        out_specs=[VMEM] * len(outs) if isinstance(outs, (list, tuple)) else VMEM,
        scratch_shapes=list(scratch),
        compiler_params=pltpu.CompilerParams(vmem_limit_bytes=LIMIT),
        cost_estimate=pl.CostEstimate(flops=flops, bytes_accessed=nbytes, transcendentals=0),
        name=name,
    )(*ins, *after)


def dft_packed(length):
    full = length // LANES * LANES
    part = np.concatenate([np.zeros(full), np.ones(full), np.zeros(length - full), np.ones(length - full)])
    index = np.concatenate([np.arange(full)] * 2 + [np.arange(full, length)] * 2)
    angle = (index[:, None] * index[None, :] % length) * (2.0 * math.pi / length)
    cosine, sine = np.cos(angle), np.sin(angle)
    same = part[:, None] == part[None, :]
    matrix = np.where(same, cosine, np.where(part[:, None] == 0, -sine, sine)) / math.sqrt(length)
    high = matrix.astype(ml_dtypes.bfloat16)
    low = (matrix - high.astype(np.float64)).astype(ml_dtypes.bfloat16)
    return high, low


def split(value):
    high = value.astype(BF16)
    return high, (value - high.astype(F32)).astype(BF16)


def dot3(high, low, mat_high, mat_low, dims):
    dot = functools.partial(lax.dot_general, dimension_numbers=(dims, ((), ())), preferred_element_type=F32)
    return dot(high, mat_high) + (dot(high, mat_low) + dot(low, mat_high))


def coil_forward_body(grad_ref, sens_ref, high_ref, low_ref, out_ref, send_ref, x_high, x_low):
    depth_len, coils, _, col_len, row_len = sens_ref.shape
    full = row_len // LANES * LANES
    count = coils * col_len
    for z in range(depth_len):
        sens_r, sens_i = sens_ref[z, :, 0], sens_ref[z, :, 1]
        img_r, img_i = grad_ref[z, 0][None], grad_ref[z, 1][None]
        real = sens_r * img_r - sens_i * img_i
        imag = sens_r * img_i + sens_i * img_r
        rest = jnp.concatenate([real[..., full:], imag[..., full:]], axis=-1)
        for piece, start in ((real[..., :full], 0), (imag[..., :full], full), (rest, 2 * full)):
            width = piece.shape[-1]
            high, low = split(piece.reshape(count, width))
            x_high[z * count : (z + 1) * count, start : start + width] = high
            x_low[z * count : (z + 1) * count, start : start + width] = low
    result = dot3(x_high[...], x_low[...], high_ref[...], low_ref[...], ((1,), (0,)))
    out_ref[...] = result
    send_ref[...] = result.astype(BF16)


def coil_backward_body(slabs, grad_ref, sens_ref, mask_ref, high_ref, low_ref, own_ref, *refs):
    others, out_ref, x_high, x_low = refs[: slabs - 1], refs[-3], refs[-2], refs[-1]
    depth_len, coils, _, col_len, row_len = sens_ref.shape
    total = slabs * depth_len
    full = row_len // LANES * LANES
    rem = row_len - full
    count = coils * col_len
    mask = mask_ref[...].astype(F32)

    def table(turn):
        real = jnp.zeros((1, row_len), F32)
        imag = jnp.zeros((1, row_len), F32)
        has_imag = False
        for kz in range(total):
            angle = 2.0 * math.pi * ((kz * turn) % total) / total
            cosine, sine = round(math.cos(angle), 15) / total, round(math.sin(angle), 15) / total
            real = real + mask[kz : kz + 1] * cosine
            if sine != 0.0:
                imag = imag + mask[kz : kz + 1] * sine
                has_imag = True
        real_rest = jnp.concatenate([real[:, full:], real[:, full:]], axis=-1)
        imag_rest = jnp.concatenate([-imag[:, full:], imag[:, full:]], axis=-1)
        return real[:, :full], imag[:, :full], real_rest, imag_rest, has_imag

    tables = {}
    for z in range(depth_len):
        sums = None
        for step in range(slabs):
            src = own_ref if step == 0 else others[step - 1]
            for zin in range(depth_len):
                turn = (step * depth_len + z - zin) % total
                if turn not in tables:
                    tables[turn] = table(turn)
                real, imag, real_rest, imag_rest, has_imag = tables[turn]
                block = src[zin * count : (zin + 1) * count, :].astype(F32)
                v_r, v_i, v_rest = block[:, :full], block[:, full : 2 * full], block[:, 2 * full :]
                if has_imag:
                    terms = (
                        real * v_r - imag * v_i,
                        real * v_i + imag * v_r,
                        real_rest * v_rest + imag_rest * pltpu.roll(v_rest, rem, 1),
                    )
                else:
                    terms = (real * v_r, real * v_i, real_rest * v_rest)
                sums = terms if sums is None else tuple(a + b for a, b in zip(sums, terms))
        for piece, start in zip(sums, (0, full, 2 * full)):
            high, low = split(piece)
            x_high[z * count : (z + 1) * count, start : start + piece.shape[1]] = high
            x_low[z * count : (z + 1) * count, start : start + piece.shape[1]] = low
    back = dot3(x_high[...], x_low[...], high_ref[...], low_ref[...], ((1,), (1,)))
    for z in range(depth_len):
        sens_r, sens_i = sens_ref[z, :, 0], sens_ref[z, :, 1]
        block = back[z * count : (z + 1) * count].reshape(coils, col_len, 2 * row_len)
        b_r, b_i, b_rest = block[..., :full], block[..., full : 2 * full], block[..., 2 * full :]
        s_r, s_i = sens_r[..., :full], sens_i[..., :full]
        out_ref[z, 0, :, :full] = grad_ref[z, 0, :, :full] - jnp.sum(s_r * b_r + s_i * b_i, axis=0)
        out_ref[z, 1, :, :full] = grad_ref[z, 1, :, :full] - jnp.sum(s_r * b_i - s_i * b_r, axis=0)
        s_rest = jnp.concatenate([sens_r[..., full:], sens_i[..., full:]], axis=-1)
        turned = pltpu.roll(b_rest, rem, 2)
        along = jnp.sum(s_rest * b_rest, axis=0)
        across = jnp.sum(s_rest * turned, axis=0)
        real = along + pltpu.roll(along, rem, 1)
        imag = across - pltpu.roll(across, rem, 1)
        out_ref[z, 0, :, full:] = grad_ref[z, 0, :, full:] - real[:, :rem]
        out_ref[z, 1, :, full:] = grad_ref[z, 1, :, full:] - imag[:, :rem]


def tap_group(scal_ref, phase_kind, flip, step_z):
    core = scal_ref[1]
    time_off = {"own": 1, "on": 2 - 2 * core, "off": 2 * core}[phase_kind]
    depth_off = jnp.where(scal_ref[0] == 1, 2 - step_z, step_z) if flip else step_z
    return 9 * time_off + 3 * depth_off


def shift_rows(value, step):
    rows = value.shape[0]
    turned = pltpu.roll(value, step % rows, 0)
    place = lax.broadcasted_iota(jnp.int32, value.shape, 0)
    return jnp.where(place == (0 if step > 0 else rows - 1), 0.0, turned)


def two_columns(weight):
    zero = jnp.zeros_like(weight)
    return jnp.concatenate(
        [jnp.concatenate([weight, zero], axis=1), jnp.concatenate([zero, weight], axis=1)], axis=0
    ).astype(BF16)


def fill_band(scal_ref, weight_ref, band, entries, outs, flip, back):
    width = LANES * len(outs)
    made = {}
    for i, (kind, place) in enumerate(entries):
        for j, out_place in enumerate(outs):
            step_z = place - out_place + 1
            for dy in range(3):
                lanes = slice(dy * width + j * LANES, dy * width + (j + 1) * LANES)
                if 0 <= step_z <= 2:
                    if (kind, step_z, dy) not in made:
                        tap = tap_group(scal_ref, kind, flip, step_z) + dy
                        weight = weight_ref[weight_ref.shape[0] - 1 - tap if back else tap].astype(F32)
                        made[kind, step_z, dy] = two_columns(weight.T if back else weight)
                    block = made[kind, step_z, dy]
                else:
                    block = jnp.zeros((LANES, LANES), BF16)
                band[i * LANES : (i + 1) * LANES, lanes] = block


def place_of(scal_ref, j, depth_len, flip):
    return jnp.where(scal_ref[0] == 1, depth_len - 1 - j, j) if flip else j


def conv_columns(refs, band, lanes):
    stacked = jnp.concatenate([ref[:, lanes] for ref in refs], axis=1)
    taps = jnp.dot(stacked, band[...], preferred_element_type=F32)
    width = taps.shape[1] // 3
    return (
        shift_rows(taps[:, :width], 1)
        + taps[:, width : 2 * width]
        + shift_rows(taps[:, 2 * width :], -1)
    )


def stack_body(*refs):
    inputs, out_ref = refs[:-1], refs[-1]
    rows, packed_len = inputs[0].shape
    for i, start in enumerate(range(0, packed_len, 2 * LANES)):
        for k, ref in enumerate(inputs):
            pair = jnp.concatenate([ref[:, start : start + LANES], ref[:, start + LANES : start + 2 * LANES]], axis=0)
            value = pair.astype(F32).T
            out_ref[k * LANES : (k + 1) * LANES, 2 * rows * i : 2 * rows * (i + 1)] = value.astype(BF16)


def conv_main_body(entries, flip, back, stacked, scal_ref, weight_ref, *refs):
    inputs, out_ref, band = refs[: len(entries)], refs[len(entries)], refs[-1]
    if stacked:
        stack_body(*[inputs[k] for k in stacked], refs[len(entries) + 1])
    depth_len = out_ref.shape[0]
    fill_band(scal_ref, weight_ref, band, entries, tuple(range(depth_len)), flip, back)
    for start in range(0, out_ref.shape[2], LANES):
        lanes = slice(start, start + LANES)
        result = conv_columns(inputs, band, lanes)
        for j in range(depth_len):
            out_ref[j, :, lanes] = result[:, j * LANES : (j + 1) * LANES]


def corner_plans(groups, flip, back, scal_ref, weight_ref, inputs, bands):
    plans = {}
    for (entries, out_place), band in zip(groups, bands):
        fill_band(scal_ref, weight_ref, band, entries, (out_place,), flip, back)
        plans[out_place] = (inputs[: len(entries)], band)
        inputs = inputs[len(entries) :]
    return plans


def grad_act_body(groups, flip, scal_ref, acc_ref, image_ref, spread_ref, weight_ref, *refs):
    depth_len, count = acc_ref.shape[0], len(groups)
    slab_in, inputs, refs = refs[:count], refs[count : 3 * count], refs[3 * count :]
    outs, ends, bands = refs[:depth_len], refs[depth_len : depth_len + count], refs[depth_len + count :]
    for k, end in enumerate(ends):
        stack_body(slab_in[k], *inputs[2 * k : 2 * k + 2], end)
    plans = corner_plans(groups, flip, False, scal_ref, weight_ref, inputs, bands)
    row_len = image_ref.shape[3]
    for j in range(depth_len):
        place = place_of(scal_ref, j, depth_len, flip)
        image = image_ref[place].reshape(-1, row_len)
        first, low = split(image)
        middle, last = split(image - first.astype(F32))
        stacked = jnp.concatenate([first, middle, last], axis=0)
        for start in range(0, acc_ref.shape[2], LANES):
            lanes = slice(start, start + LANES)
            grad_silu = lax.dot_general(
                stacked, spread_ref[:, lanes], (((0,), (0,)), ((), ())), preferred_element_type=F32
            )
            act = acc_ref[j, :, lanes]
            if j in plans:
                act = act + conv_columns(*plans[j], lanes)
            gate = 0.5 * jnp.tanh(0.5 * act) + 0.5
            outs[j][:, lanes] = (grad_silu * (gate * (1.0 + act * (1.0 - gate)))).astype(BF16)


def grad_feature_body(groups, flip, scal_ref, acc_ref, weight_ref, *refs):
    inputs, out_ref, bands = refs[: 2 * len(groups)], refs[2 * len(groups)], refs[2 * len(groups) + 1 :]
    plans = corner_plans(groups, flip, True, scal_ref, weight_ref, inputs, bands)
    depth_len = acc_ref.shape[0]
    for j in range(depth_len):
        place = jnp.where(scal_ref[0] == 1, depth_len - 1 - j, j) if flip else j
        for start in range(0, acc_ref.shape[2], LANES):
            lanes = slice(start, start + LANES)
            total = acc_ref[j, :, lanes]
            if j in plans:
                total = total + conv_columns(*plans[j], lanes)
            out_ref[place, :, lanes] = total.astype(BF16)


def reach(place, outs):
    return [j for j, out_place in enumerate(outs) if 0 <= place - out_place + 1 <= 2]


def grad_weight_body(groups, outs, flip, scal_ref, *refs):
    n_out = len(outs)
    keep_ref, send_ref, right, packed = refs[-4:]
    stacks, grads = refs[: -4 - n_out], refs[-4 - n_out : -4]
    rows, packed_len = grads[0].shape
    half = LANES // 2
    width = 3 * LANES
    for i, start in enumerate(range(0, packed_len, LANES)):
        lanes = slice(start, start + LANES)
        span = slice(i * rows, (i + 1) * rows)
        for j, ref in enumerate(grads):
            value = ref[:, lanes].astype(F32)
            at = j * width
            right[span, at : at + LANES] = shift_rows(value, -1).astype(BF16)
            right[span, at + LANES : at + 2 * LANES] = ref[:, lanes]
            right[span, at + 2 * LANES : at + 3 * LANES] = shift_rows(value, 1).astype(BF16)
    entries, rows_of = [], []
    for stack, group in zip(stacks, groups):
        near = reach(group[0][1], outs)
        part = jnp.dot(
            stack[...], right[:, near[0] * width : (near[-1] + 1) * width], preferred_element_type=F32
        )
        for k, entry in enumerate(group):
            entries.append(entry)
            rows_of.append({
                j: part[k * LANES : (k + 1) * LANES, (j - near[0]) * width : (j - near[0] + 1) * width] for j in near
            })
    quarter = half // 2
    lane = lax.broadcasted_iota(jnp.int32, (quarter, LANES), 1)
    packed[27 * quarter :] = jnp.zeros((packed.shape[0] - 27 * quarter, LANES), F32)
    for kind in ("own", "on", "off"):
        for step_z in range(3):
            for dy in range(3):
                total = None
                for k, (this, place) in enumerate(entries):
                    for j, out_place in enumerate(outs):
                        if this == kind and place - out_place + 1 == step_z:
                            block = rows_of[k][j][:, dy * LANES : (dy + 1) * LANES]
                            total = block if total is None else total + block
                direct = jnp.where(lane < half, total[:quarter], total[3 * quarter :])
                turned = jnp.where(lane < half, total[quarter : 2 * quarter], total[2 * quarter : 3 * quarter])
                tap = tap_group(scal_ref, kind, flip, step_z) + dy
                packed[pl.ds(pl.multiple_of(tap * quarter, quarter), quarter), :] = direct + pltpu.roll(turned, half, 1)
    share = packed.shape[0] // 2
    core = scal_ref[1]
    keep_ref[...] = packed[pl.ds(pl.multiple_of(core * share, quarter), share), :]
    send_ref[...] = packed[pl.ds(pl.multiple_of((1 - core) * share, quarter), share), :]


def unpack_body(where_ref, *refs):
    pieces, out_ref, packed = refs[:-2], refs[-2], refs[-1]
    share = pieces[0].shape[0]
    for i, ref in enumerate(pieces):
        packed[where_ref[i]] = ref[...].astype(F32)
    flat = packed[...].reshape(-1, LANES)
    taps, height, _ = out_ref.shape
    quarter = height // 2
    for tap in range(taps):
        block = flat[tap * quarter : (tap + 1) * quarter]
        out_ref[tap, :quarter, :] = block[:, : LANES // 2]
        out_ref[tap, quarter:, :] = pltpu.roll(block, LANES // 2, 1)[:, : LANES // 2]


def final_body(groups, flip, scal_ref, acc_ref, weight_ref, *refs):
    corners, count = refs[: 2 * len(groups)], 2 * len(groups)
    where_ref, pieces = refs[count], refs[count + 1 : count + 5]
    features_ref, taps_ref, packed, bands = refs[count + 5], refs[count + 6], refs[-1], refs[count + 7 : -1]
    unpack_body(where_ref, *pieces, taps_ref, packed)
    grad_feature_body(groups, flip, scal_ref, acc_ref, weight_ref, *corners, features_ref, *bands)


def pair_on(size):
    return [(i, i ^ 1) for i in range(size)]


def pair_off(size):
    return [(i, (i - 1) % size if i % 2 == 0 else (i + 1) % size) for i in range(size)]


def fold_body(pick_ref, keep_ref, got_ref, own_ref, send_ref):
    rows = own_ref.shape[0]
    for spot, out_ref in ((pick_ref[0], own_ref), (1 - pick_ref[0], send_ref)):
        span = pl.ds(pl.multiple_of(spot * rows, rows), rows)
        out_ref[...] = keep_ref[span, :] + got_ref[span, :]


def round_body(value_ref, got_ref, out_ref):
    out_ref[...] = (value_ref[...] + got_ref[...]).astype(out_ref.dtype)


def exchanges(axis, stride, size, total):
    return [(axis, [(i, i ^ (stride * bit)) for i in range(total)]) for bit in (1 << k for k in range(size.bit_length() - 1))]


def sum_over_mesh(keep, send, phases, slabs, after_finish):
    phase = lax.axis_index("phase")
    core, column = phase % 2, phase // 2 % 2
    part_shape = (keep.shape[0] // 2, LANES)
    across = [(p, p ^ 2) for p in range(phases)]
    part, other = call(
        "fold",
        fold_body,
        [jax.ShapeDtypeStruct(part_shape, F32)] * 2,
        (column.reshape(1), keep, lax.ppermute(send, "phase", pair_on(phases))),
        "SVV",
        nbytes=100000,
    )
    part = part + lax.ppermute(other, "phase", across)
    steps = exchanges("slab", 1, slabs, slabs) + exchanges("phase", 4, phases // 4, phases)
    for axis, perm in steps[:-1]:
        part = part + lax.ppermute(part, axis, perm)
    axis, perm = steps[-1]
    part = call(
        "finish",
        round_body,
        jax.ShapeDtypeStruct(part_shape, BF16),
        (part, lax.ppermute(part, axis, perm)),
        "VV",
        nbytes=30000,
        after=after_finish,
    )
    pieces = [part, lax.ppermute(part, "phase", across)]
    pieces += [lax.ppermute(piece, "phase", pair_on(phases)) for piece in pieces]
    spots = [2 * core + column, 2 * core + 1 - column]
    spots += [2 * (1 - core) + column, 2 * (1 - core) + 1 - column]
    return pieces, jnp.stack(spots).astype(jnp.int32)


def local(phases, slabs, features, conv_weight, projection, grad_out, sens, mask):
    _, depth_len, row_len, packed_len = features.shape
    channels = conv_weight.shape[1]
    col_len = packed_len // channels
    coils = sens.shape[1]
    taps = conv_weight.shape[0]
    slab, core = lax.axis_index("slab"), lax.axis_index("phase") % 2
    flip = slabs == 2
    scal = jnp.stack([slab, core]).astype(jnp.int32)
    on, off = pair_on(phases), pair_off(phases)

    def pass_phase(value, perm):
        return lax.ppermute(value, "phase", perm)

    if flip:
        order = list(range(depth_len))
        edges = [(depth_len - 1, depth_len, [(0, 1), (1, 0)])]
        pick = lambda j: jnp.where(slab == 1, depth_len - 1 - j, j)
    else:
        order = list(range(depth_len))
        up = [(i, i + 1) for i in range(slabs - 1)]
        edges = [(depth_len - 1, -1, up), (0, depth_len, [(j, i) for i, j in up])]
        pick = lambda j: j

    first_sent = [edge[0] for edge in edges]

    def halo(own):
        off_in = {}
        for j in first_sent + [j for j in order if j not in first_sent]:
            off_in[j] = pass_phase(own[j], off)
        slab_in = [lax.ppermute(own[edge[0]], "slab", edge[2]) for edge in edges]
        on_in = [pass_phase(own[j], on) for j in order]
        corner_off = [lax.ppermute(off_in[edge[0]], "slab", edge[2]) for edge in edges]
        corner_on = [pass_phase(value, on) for value in slab_in]
        corners = []
        for a, b in zip(corner_off, corner_on):
            corners += [a, b]
        full = list(own) + on_in + [off_in[j] for j in order]
        ends = [list(values) for values in zip(slab_in, corner_off, corner_on)]
        return full, full + slab_in, corners, ends

    main_entries = (
        [(kind, j) for kind in ("own", "on", "off") for j in order] + [("own", edge[1]) for edge in edges]
    )
    corner_entries = []
    corner_groups = []
    for edge in edges:
        near = min(max(edge[1], 0), depth_len - 1)
        corner_groups.append(([("off", edge[1]), ("on", edge[1])], near))
        corner_entries += [("off", edge[1]), ("on", edge[1])]
    corner_groups.sort(key=lambda g: g[1])

    high, low = dft_packed(row_len)
    high, low = jnp.asarray(high), jnp.asarray(low)
    lines = depth_len * coils * col_len
    grad_now = grad_out[0]
    line_shape = (lines, 2 * row_len)
    slice_shape = (row_len, packed_len)
    slab_shape = (depth_len, row_len, packed_len)
    scratch = [pltpu.VMEM(line_shape, BF16)] * 2
    coil_flops = 3 * 2 * lines * (2 * row_len) ** 2
    own_lines, sent_lines = call(
        "coil_forward",
        coil_forward_body,
        [jax.ShapeDtypeStruct(line_shape, F32), jax.ShapeDtypeStruct(line_shape, BF16)],
        (grad_now, sens, high, low),
        "VHHH",
        scratch=scratch,
        flops=coil_flops,
        nbytes=4000000,
    )
    own_slices = [lax.dynamic_index_in_dim(features[0], pick(j), 0, keepdims=False) for j in order]
    full_in, main_in, corner_in, ends_in = halo(own_slices)
    sent_lines, _ = lax.optimization_barrier((sent_lines, full_in[depth_len : 2 * depth_len]))
    other_lines = [
        lax.ppermute(sent_lines, "slab", [(i, (i + k) % slabs) for i in range(slabs)]) for k in range(1, slabs)
    ]
    spread = -(projection[:, None, None, :] * jnp.eye(col_len, dtype=BF16)[None, :, :, None])
    spread = spread.reshape(2 * col_len, packed_len)
    spread = jnp.concatenate([spread] * 3, axis=0)

    bands = [pltpu.VMEM((len(g[0]) * LANES, 3 * LANES), BF16) for g in corner_groups]

    conv_flops = 2 * row_len * len(main_entries) * packed_len * 3 * depth_len * LANES
    small_flops = 2 * row_len * 2 * packed_len * 3 * LANES

    def conv_main(name, back, inputs, after=(), stacked=()):
        return call(
            name,
            functools.partial(conv_main_body, main_entries, flip, back, stacked),
            [jax.ShapeDtypeStruct(slab_shape, F32)]
            + [jax.ShapeDtypeStruct((len(stacked) * LANES, packed_len // LANES * row_len), BF16)] * bool(stacked),
            (scal, conv_weight, *inputs),
            "SV" + "V" * len(inputs),
            scratch=[pltpu.VMEM((len(main_entries) * LANES, 3 * depth_len * LANES), BF16)],
            flops=conv_flops,
            nbytes=5000000,
            after=after,
        )

    whole = tuple(range(3 * depth_len))
    acc, stack_full = conv_main("conv_act", False, main_in, (), whole)
    grad_image = call(
        "coil_back",
        functools.partial(coil_backward_body, slabs),
        jax.ShapeDtypeStruct(grad_now.shape, F32),
        (grad_now, sens, mask[0], high, low, own_lines, *other_lines),
        "VVVVVV" + "V" * len(other_lines),
        after=[acc],
        scratch=scratch,
        flops=coil_flops,
        nbytes=5000000,
    )

    grad_outs = call(
        "grad_act",
        functools.partial(grad_act_body, corner_groups, flip),
        [pltpu.VMEM(slice_shape, BF16)] * depth_len
        + [pltpu.VMEM((3 * LANES, packed_len // LANES * row_len), BF16)] * len(edges),
        (scal, acc, grad_image, spread, conv_weight, *[values[0] for values in ends_in], *corner_in),
        "SVHVV" + "V" * (len(edges) + len(corner_in)),
        flops=small_flops,
        nbytes=4000000,
        scratch=bands,
        after=[],
    )

    grad_act, stack_ends = grad_outs[:depth_len], grad_outs[depth_len:]
    _, main_grad, corner_grad, _ = halo(grad_act)

    share = (taps + 1) // 2 * channels // 2
    stacks = [stack_full, *stack_ends]
    weight_groups = [[(kind, j) for kind in ("own", "on", "off") for j in order]]
    weight_groups += [[(kind, edge[1]) for kind in ("own", "off", "on")] for edge in edges]
    keep, send = call(
        "grad_weight",
        functools.partial(grad_weight_body, weight_groups, tuple(order), flip),
        [jax.ShapeDtypeStruct((share, LANES), F32)] * 2,
        (scal, *stacks, *grad_act),
        "SV" + "M" * (len(stacks) - 1 + depth_len),
        after=[],
        scratch=[
            pltpu.VMEM((packed_len // LANES * row_len, 3 * depth_len * LANES), BF16),
            pltpu.VMEM((2 * share, LANES), F32),
        ],
        flops=conv_flops,
        nbytes=5000000,
    )

    (acc_back,) = conv_main("conv_back", True, main_grad)
    pieces, spots = sum_over_mesh(keep, send, phases, slabs, [acc_back])
    grad_features, grad_weight = call(
        "finish_both",
        functools.partial(final_body, corner_groups, flip),
        [jax.ShapeDtypeStruct(slab_shape, BF16), jax.ShapeDtypeStruct(conv_weight.shape, F32)],
        (scal, acc_back, conv_weight, *corner_grad, spots, *pieces),
        "SVV" + "V" * len(corner_grad) + "S" + "V" * len(pieces),
        scratch=bands + [pltpu.VMEM((len(pieces),) + pieces[0].shape, F32)],
        flops=small_flops,
        nbytes=4000000,
    )
    return (grad_image[None], grad_features[None], grad_weight)


def solution(mesh):
    in_specs = (
        P("phase", "slab", None, None),
        P(),
        P(),
        P("phase", "slab", None, None, None),
        P("slab", None, None, None, None),
        P("phase", None, None),
    )
    out_specs = (P("phase", "slab", None, None, None), P("phase", "slab", None, None), P())
    body = functools.partial(local, mesh.shape["phase"], mesh.shape["slab"])
    return jax.shard_map(body, mesh=mesh, in_specs=in_specs, out_specs=out_specs, check_vma=False)
```

```python
import functools
import math

import jax
import jax.numpy as jnp
import ml_dtypes
import numpy as np
from jax import lax
from jax.experimental import pallas as pl
from jax.experimental.pallas import tpu as pltpu
from jax.sharding import PartitionSpec as P

F32, BF16 = jnp.float32, jnp.bfloat16
VMEM = pl.BlockSpec(memory_space=pltpu.VMEM)
SMEM = pl.BlockSpec(memory_space=pltpu.SMEM)
LIMIT = 48 * 1024 * 1024
LANES = 128


ANY = pl.BlockSpec(memory_space=pl.ANY)
SPECS = {"S": SMEM, "V": VMEM, "M": VMEM, "H": VMEM}


def call(name, body, outs, ins, kinds, scratch=(), flops=0, nbytes=0, after=()):
    count, waits = len(ins), len(after)

    def run(*refs):
        body(*refs[:count], *refs[count + waits :])

    spaces = {"M": pltpu.VMEM, "H": pltpu.HBM}
    ins = [
        pltpu.with_memory_space_constraint(x, spaces[kind]) if kind in spaces else x for x, kind in zip(ins, kinds)
    ]
    return pl.pallas_call(
        run,
        out_shape=outs,
        in_specs=[SPECS[kind] for kind in kinds] + [ANY] * waits,
        out_specs=[VMEM] * len(outs) if isinstance(outs, (list, tuple)) else VMEM,
        scratch_shapes=list(scratch),
        compiler_params=pltpu.CompilerParams(vmem_limit_bytes=LIMIT),
        cost_estimate=pl.CostEstimate(flops=flops, bytes_accessed=nbytes, transcendentals=0),
        name=name,
    )(*ins, *after)


def dft_packed(length):
    full = length // LANES * LANES
    part = np.concatenate([np.zeros(full), np.ones(full), np.zeros(length - full), np.ones(length - full)])
    index = np.concatenate([np.arange(full)] * 2 + [np.arange(full, length)] * 2)
    angle = (index[:, None] * index[None, :] % length) * (2.0 * math.pi / length)
    cosine, sine = np.cos(angle), np.sin(angle)
    same = part[:, None] == part[None, :]
    matrix = np.where(same, cosine, np.where(part[:, None] == 0, -sine, sine)) / math.sqrt(length)
    high = matrix.astype(ml_dtypes.bfloat16)
    low = (matrix - high.astype(np.float64)).astype(ml_dtypes.bfloat16)
    return high, low


def split(value):
    high = value.astype(BF16)
    return high, (value - high.astype(F32)).astype(BF16)


def dot3(high, low, mat_high, mat_low, dims):
    dot = functools.partial(lax.dot_general, dimension_numbers=(dims, ((), ())), preferred_element_type=F32)
    return dot(high, mat_high) + (dot(high, mat_low) + dot(low, mat_high))


def coil_forward_body(grad_ref, sens_ref, high_ref, low_ref, out_ref, send_ref, x_high, x_low):
    depth_len, coils, _, col_len, row_len = sens_ref.shape
    full = row_len // LANES * LANES
    count = coils * col_len
    for z in range(depth_len):
        sens_r, sens_i = sens_ref[z, :, 0], sens_ref[z, :, 1]
        img_r, img_i = grad_ref[z, 0][None], grad_ref[z, 1][None]
        real = sens_r * img_r - sens_i * img_i
        imag = sens_r * img_i + sens_i * img_r
        rest = jnp.concatenate([real[..., full:], imag[..., full:]], axis=-1)
        for piece, start in ((real[..., :full], 0), (imag[..., :full], full), (rest, 2 * full)):
            width = piece.shape[-1]
            high, low = split(piece.reshape(count, width))
            x_high[z * count : (z + 1) * count, start : start + width] = high
            x_low[z * count : (z + 1) * count, start : start + width] = low
    result = dot3(x_high[...], x_low[...], high_ref[...], low_ref[...], ((1,), (0,)))
    out_ref[...] = result
    send_ref[...] = result.astype(BF16)


def coil_backward_body(slabs, grad_ref, sens_ref, mask_ref, high_ref, low_ref, own_ref, *refs):
    others, out_ref, x_high, x_low = refs[: slabs - 1], refs[-3], refs[-2], refs[-1]
    depth_len, coils, _, col_len, row_len = sens_ref.shape
    total = slabs * depth_len
    full = row_len // LANES * LANES
    rem = row_len - full
    count = coils * col_len
    mask = mask_ref[...].astype(F32)

    def table(turn):
        real = jnp.zeros((1, row_len), F32)
        imag = jnp.zeros((1, row_len), F32)
        has_imag = False
        for kz in range(total):
            angle = 2.0 * math.pi * ((kz * turn) % total) / total
            cosine, sine = round(math.cos(angle), 15) / total, round(math.sin(angle), 15) / total
            real = real + mask[kz : kz + 1] * cosine
            if sine != 0.0:
                imag = imag + mask[kz : kz + 1] * sine
                has_imag = True
        real_rest = jnp.concatenate([real[:, full:], real[:, full:]], axis=-1)
        imag_rest = jnp.concatenate([-imag[:, full:], imag[:, full:]], axis=-1)
        return real[:, :full], imag[:, :full], real_rest, imag_rest, has_imag

    tables = {}
    for z in range(depth_len):
        sums = None
        for step in range(slabs):
            src = own_ref if step == 0 else others[step - 1]
            for zin in range(depth_len):
                turn = (step * depth_len + z - zin) % total
                if turn not in tables:
                    tables[turn] = table(turn)
                real, imag, real_rest, imag_rest, has_imag = tables[turn]
                block = src[zin * count : (zin + 1) * count, :].astype(F32)
                v_r, v_i, v_rest = block[:, :full], block[:, full : 2 * full], block[:, 2 * full :]
                if has_imag:
                    terms = (
                        real * v_r - imag * v_i,
                        real * v_i + imag * v_r,
                        real_rest * v_rest + imag_rest * pltpu.roll(v_rest, rem, 1),
                    )
                else:
                    terms = (real * v_r, real * v_i, real_rest * v_rest)
                sums = terms if sums is None else tuple(a + b for a, b in zip(sums, terms))
        for piece, start in zip(sums, (0, full, 2 * full)):
            high, low = split(piece)
            x_high[z * count : (z + 1) * count, start : start + piece.shape[1]] = high
            x_low[z * count : (z + 1) * count, start : start + piece.shape[1]] = low
    back = dot3(x_high[...], x_low[...], high_ref[...], low_ref[...], ((1,), (1,)))
    for z in range(depth_len):
        sens_r, sens_i = sens_ref[z, :, 0], sens_ref[z, :, 1]
        block = back[z * count : (z + 1) * count].reshape(coils, col_len, 2 * row_len)
        b_r, b_i, b_rest = block[..., :full], block[..., full : 2 * full], block[..., 2 * full :]
        s_r, s_i = sens_r[..., :full], sens_i[..., :full]
        out_ref[z, 0, :, :full] = grad_ref[z, 0, :, :full] - jnp.sum(s_r * b_r + s_i * b_i, axis=0)
        out_ref[z, 1, :, :full] = grad_ref[z, 1, :, :full] - jnp.sum(s_r * b_i - s_i * b_r, axis=0)
        s_rest = jnp.concatenate([sens_r[..., full:], sens_i[..., full:]], axis=-1)
        turned = pltpu.roll(b_rest, rem, 2)
        along = jnp.sum(s_rest * b_rest, axis=0)
        across = jnp.sum(s_rest * turned, axis=0)
        real = along + pltpu.roll(along, rem, 1)
        imag = across - pltpu.roll(across, rem, 1)
        out_ref[z, 0, :, full:] = grad_ref[z, 0, :, full:] - real[:, :rem]
        out_ref[z, 1, :, full:] = grad_ref[z, 1, :, full:] - imag[:, :rem]


def tap_group(scal_ref, phase_kind, flip, step_z):
    core = scal_ref[1]
    time_off = {"own": 1, "on": 2 - 2 * core, "off": 2 * core}[phase_kind]
    depth_off = jnp.where(scal_ref[0] == 1, 2 - step_z, step_z) if flip else step_z
    return 9 * time_off + 3 * depth_off


def shift_rows(value, step):
    rows = value.shape[0]
    turned = pltpu.roll(value, step % rows, 0)
    place = lax.broadcasted_iota(jnp.int32, value.shape, 0)
    return jnp.where(place == (0 if step > 0 else rows - 1), 0.0, turned)


def two_columns(weight):
    zero = jnp.zeros_like(weight)
    return jnp.concatenate(
        [jnp.concatenate([weight, zero], axis=1), jnp.concatenate([zero, weight], axis=1)], axis=0
    ).astype(BF16)


def fill_band(scal_ref, weight_ref, band, entries, outs, flip, back):
    width = LANES * len(outs)
    made = {}
    for i, (kind, place) in enumerate(entries):
        for j, out_place in enumerate(outs):
            step_z = place - out_place + 1
            for dy in range(3):
                lanes = slice(dy * width + j * LANES, dy * width + (j + 1) * LANES)
                if 0 <= step_z <= 2:
                    if (kind, step_z, dy) not in made:
                        tap = tap_group(scal_ref, kind, flip, step_z) + dy
                        weight = weight_ref[weight_ref.shape[0] - 1 - tap if back else tap].astype(F32)
                        made[kind, step_z, dy] = two_columns(weight.T if back else weight)
                    block = made[kind, step_z, dy]
                else:
                    block = jnp.zeros((LANES, LANES), BF16)
                band[i * LANES : (i + 1) * LANES, lanes] = block


def place_of(scal_ref, j, depth_len, flip):
    return jnp.where(scal_ref[0] == 1, depth_len - 1 - j, j) if flip else j


def conv_columns(refs, band, lanes):
    stacked = jnp.concatenate([ref[:, lanes] for ref in refs], axis=1)
    taps = jnp.dot(stacked, band[...], preferred_element_type=F32)
    width = taps.shape[1] // 3
    return (
        shift_rows(taps[:, :width], 1)
        + taps[:, width : 2 * width]
        + shift_rows(taps[:, 2 * width :], -1)
    )


def stack_body(*refs):
    inputs, out_ref = refs[:-1], refs[-1]
    rows, packed_len = inputs[0].shape
    for i, start in enumerate(range(0, packed_len, 2 * LANES)):
        for k, ref in enumerate(inputs):
            pair = jnp.concatenate([ref[:, start : start + LANES], ref[:, start + LANES : start + 2 * LANES]], axis=0)
            value = pair.astype(F32).T
            out_ref[k * LANES : (k + 1) * LANES, 2 * rows * i : 2 * rows * (i + 1)] = value.astype(BF16)


def conv_main_body(entries, flip, back, stacked, scal_ref, weight_ref, *refs):
    inputs, out_ref, band = refs[: len(entries)], refs[len(entries)], refs[-1]
    if stacked:
        stack_body(*[inputs[k] for k in stacked], refs[len(entries) + 1])
    depth_len = out_ref.shape[0]
    fill_band(scal_ref, weight_ref, band, entries, tuple(range(depth_len)), flip, back)
    for start in range(0, out_ref.shape[2], LANES):
        lanes = slice(start, start + LANES)
        result = conv_columns(inputs, band, lanes)
        for j in range(depth_len):
            out_ref[j, :, lanes] = result[:, j * LANES : (j + 1) * LANES]


def corner_plans(groups, flip, back, scal_ref, weight_ref, inputs, bands):
    plans = {}
    for (entries, out_place), band in zip(groups, bands):
        fill_band(scal_ref, weight_ref, band, entries, (out_place,), flip, back)
        plans[out_place] = (inputs[: len(entries)], band)
        inputs = inputs[len(entries) :]
    return plans


def grad_act_body(groups, flip, scal_ref, acc_ref, image_ref, spread_ref, weight_ref, *refs):
    depth_len, count = acc_ref.shape[0], len(groups)
    slab_in, inputs, refs = refs[:count], refs[count : 3 * count], refs[3 * count :]
    outs, ends, bands = refs[:depth_len], refs[depth_len : depth_len + count], refs[depth_len + count :]
    for k, end in enumerate(ends):
        stack_body(slab_in[k], *inputs[2 * k : 2 * k + 2], end)
    plans = corner_plans(groups, flip, False, scal_ref, weight_ref, inputs, bands)
    row_len = image_ref.shape[3]
    for j in range(depth_len):
        place = place_of(scal_ref, j, depth_len, flip)
        image = image_ref[place].reshape(-1, row_len)
        first, low = split(image)
        middle, last = split(image - first.astype(F32))
        stacked = jnp.concatenate([first, middle, last], axis=0)
        for start in range(0, acc_ref.shape[2], LANES):
            lanes = slice(start, start + LANES)
            grad_silu = lax.dot_general(
                stacked, spread_ref[:, lanes], (((0,), (0,)), ((), ())), preferred_element_type=F32
            )
            act = acc_ref[j, :, lanes]
            if j in plans:
                act = act + conv_columns(*plans[j], lanes)
            gate = 0.5 * jnp.tanh(0.5 * act) + 0.5
            outs[j][:, lanes] = (grad_silu * (gate * (1.0 + act * (1.0 - gate)))).astype(BF16)


def grad_feature_body(groups, flip, scal_ref, acc_ref, weight_ref, *refs):
    inputs, out_ref, bands = refs[: 2 * len(groups)], refs[2 * len(groups)], refs[2 * len(groups) + 1 :]
    plans = corner_plans(groups, flip, True, scal_ref, weight_ref, inputs, bands)
    depth_len = acc_ref.shape[0]
    for j in range(depth_len):
        place = jnp.where(scal_ref[0] == 1, depth_len - 1 - j, j) if flip else j
        for start in range(0, acc_ref.shape[2], LANES):
            lanes = slice(start, start + LANES)
            total = acc_ref[j, :, lanes]
            if j in plans:
                total = total + conv_columns(*plans[j], lanes)
            out_ref[place, :, lanes] = total.astype(BF16)


def reach(place, outs):
    return [j for j, out_place in enumerate(outs) if 0 <= place - out_place + 1 <= 2]


def grad_weight_body(groups, outs, flip, scal_ref, *refs):
    n_out = len(outs)
    keep_ref, send_ref, right, packed = refs[-4:]
    stacks, grads = refs[: -4 - n_out], refs[-4 - n_out : -4]
    rows, packed_len = grads[0].shape
    half = LANES // 2
    width = 3 * LANES
    for i, start in enumerate(range(0, packed_len, LANES)):
        lanes = slice(start, start + LANES)
        span = slice(i * rows, (i + 1) * rows)
        for j, ref in enumerate(grads):
            value = ref[:, lanes].astype(F32)
            at = j * width
            right[span, at : at + LANES] = shift_rows(value, -1).astype(BF16)
            right[span, at + LANES : at + 2 * LANES] = ref[:, lanes]
            right[span, at + 2 * LANES : at + 3 * LANES] = shift_rows(value, 1).astype(BF16)
    entries, rows_of = [], []
    for stack, group in zip(stacks, groups):
        near = reach(group[0][1], outs)
        part = jnp.dot(
            stack[...], right[:, near[0] * width : (near[-1] + 1) * width], preferred_element_type=F32
        )
        for k, entry in enumerate(group):
            entries.append(entry)
            rows_of.append({
                j: part[k * LANES : (k + 1) * LANES, (j - near[0]) * width : (j - near[0] + 1) * width] for j in near
            })
    quarter = half // 2
    lane = lax.broadcasted_iota(jnp.int32, (quarter, LANES), 1)
    packed[27 * quarter :] = jnp.zeros((packed.shape[0] - 27 * quarter, LANES), F32)
    for kind in ("own", "on", "off"):
        for step_z in range(3):
            for dy in range(3):
                total = None
                for k, (this, place) in enumerate(entries):
                    for j, out_place in enumerate(outs):
                        if this == kind and place - out_place + 1 == step_z:
                            block = rows_of[k][j][:, dy * LANES : (dy + 1) * LANES]
                            total = block if total is None else total + block
                direct = jnp.where(lane < half, total[:quarter], total[3 * quarter :])
                turned = jnp.where(lane < half, total[quarter : 2 * quarter], total[2 * quarter : 3 * quarter])
                tap = tap_group(scal_ref, kind, flip, step_z) + dy
                packed[pl.ds(pl.multiple_of(tap * quarter, quarter), quarter), :] = direct + pltpu.roll(turned, half, 1)
    share = packed.shape[0] // 2
    core = scal_ref[1]
    keep_ref[...] = packed[pl.ds(pl.multiple_of(core * share, quarter), share), :]
    send_ref[...] = packed[pl.ds(pl.multiple_of((1 - core) * share, quarter), share), :]


def unpack_body(where_ref, *refs):
    pieces, out_ref, packed = refs[:-2], refs[-2], refs[-1]
    share = pieces[0].shape[0]
    for i, ref in enumerate(pieces):
        packed[where_ref[i]] = ref[...].astype(F32)
    flat = packed[...].reshape(-1, LANES)
    taps, height, _ = out_ref.shape
    quarter = height // 2
    for tap in range(taps):
        block = flat[tap * quarter : (tap + 1) * quarter]
        out_ref[tap, :quarter, :] = block[:, : LANES // 2]
        out_ref[tap, quarter:, :] = pltpu.roll(block, LANES // 2, 1)[:, : LANES // 2]


def final_body(groups, flip, scal_ref, acc_ref, weight_ref, *refs):
    corners, count = refs[: 2 * len(groups)], 2 * len(groups)
    where_ref, pieces = refs[count], refs[count + 1 : count + 5]
    features_ref, taps_ref, packed, bands = refs[count + 5], refs[count + 6], refs[-1], refs[count + 7 : -1]
    unpack_body(where_ref, *pieces, taps_ref, packed)
    grad_feature_body(groups, flip, scal_ref, acc_ref, weight_ref, *corners, features_ref, *bands)


def pair_on(size):
    return [(i, i ^ 1) for i in range(size)]


def pair_off(size):
    return [(i, (i - 1) % size if i % 2 == 0 else (i + 1) % size) for i in range(size)]


def fold_body(pick_ref, keep_ref, got_ref, own_ref, send_ref):
    rows = own_ref.shape[0]
    for spot, out_ref in ((pick_ref[0], own_ref), (1 - pick_ref[0], send_ref)):
        span = pl.ds(pl.multiple_of(spot * rows, rows), rows)
        out_ref[...] = keep_ref[span, :] + got_ref[span, :]


def round_body(value_ref, got_ref, out_ref):
    out_ref[...] = (value_ref[...] + got_ref[...]).astype(out_ref.dtype)


def exchanges(axis, stride, size, total):
    return [(axis, [(i, i ^ (stride * bit)) for i in range(total)]) for bit in (1 << k for k in range(size.bit_length() - 1))]


def sum_over_mesh(keep, send, phases, slabs, after_finish):
    phase = lax.axis_index("phase")
    core, column = phase % 2, phase // 2 % 2
    part_shape = (keep.shape[0] // 2, LANES)
    across = [(p, p ^ 2) for p in range(phases)]
    part, other = call(
        "fold",
        fold_body,
        [jax.ShapeDtypeStruct(part_shape, F32)] * 2,
        (column.reshape(1), keep, lax.ppermute(send, "phase", pair_on(phases))),
        "SVV",
        nbytes=100000,
    )
    part = part + lax.ppermute(other, "phase", across)
    steps = exchanges("slab", 1, slabs, slabs) + exchanges("phase", 4, phases // 4, phases)
    for axis, perm in steps[:-1]:
        part = part + lax.ppermute(part, axis, perm)
    late = part
    axis, perm = steps[-1]
    part = call(
        "finish",
        round_body,
        jax.ShapeDtypeStruct(part_shape, BF16),
        (part, lax.ppermute(part, axis, perm)),
        "VV",
        nbytes=30000,
        after=after_finish,
    )
    pieces = [part, lax.ppermute(part, "phase", across)]
    pieces += [lax.ppermute(piece, "phase", pair_on(phases)) for piece in pieces]
    spots = [2 * core + column, 2 * core + 1 - column]
    spots += [2 * (1 - core) + column, 2 * (1 - core) + 1 - column]
    return pieces, jnp.stack(spots).astype(jnp.int32), late


def local(phases, slabs, features, conv_weight, projection, grad_out, sens, mask):
    _, depth_len, row_len, packed_len = features.shape
    channels = conv_weight.shape[1]
    col_len = packed_len // channels
    coils = sens.shape[1]
    taps = conv_weight.shape[0]
    slab, core = lax.axis_index("slab"), lax.axis_index("phase") % 2
    flip = slabs == 2
    scal = jnp.stack([slab, core]).astype(jnp.int32)
    on, off = pair_on(phases), pair_off(phases)

    def pass_phase(value, perm):
        return lax.ppermute(value, "phase", perm)

    if flip:
        order = list(range(depth_len))
        edges = [(depth_len - 1, depth_len, [(0, 1), (1, 0)])]
        pick = lambda j: jnp.where(slab == 1, depth_len - 1 - j, j)
    else:
        order = list(range(depth_len))
        up = [(i, i + 1) for i in range(slabs - 1)]
        edges = [(depth_len - 1, -1, up), (0, depth_len, [(j, i) for i, j in up])]
        pick = lambda j: j

    first_sent = [edge[0] for edge in edges]

    def halo(own):
        off_in = {}
        for j in first_sent + [j for j in order if j not in first_sent]:
            off_in[j] = pass_phase(own[j], off)
        slab_in = [lax.ppermute(own[edge[0]], "slab", edge[2]) for edge in edges]
        on_in = [pass_phase(own[j], on) for j in order]
        corner_off = [lax.ppermute(off_in[edge[0]], "slab", edge[2]) for edge in edges]
        corner_on = [pass_phase(value, on) for value in slab_in]
        corners = []
        for a, b in zip(corner_off, corner_on):
            corners += [a, b]
        full = list(own) + on_in + [off_in[j] for j in order]
        ends = [list(values) for values in zip(slab_in, corner_off, corner_on)]
        return full, full + slab_in, corners, ends

    main_entries = (
        [(kind, j) for kind in ("own", "on", "off") for j in order] + [("own", edge[1]) for edge in edges]
    )
    corner_entries = []
    corner_groups = []
    for edge in edges:
        near = min(max(edge[1], 0), depth_len - 1)
        corner_groups.append(([("off", edge[1]), ("on", edge[1])], near))
        corner_entries += [("off", edge[1]), ("on", edge[1])]
    corner_groups.sort(key=lambda g: g[1])

    high, low = dft_packed(row_len)
    high, low = jnp.asarray(high), jnp.asarray(low)
    lines = depth_len * coils * col_len
    grad_now = grad_out[0]
    line_shape = (lines, 2 * row_len)
    slice_shape = (row_len, packed_len)
    slab_shape = (depth_len, row_len, packed_len)
    scratch = [pltpu.VMEM(line_shape, BF16)] * 2
    coil_flops = 3 * 2 * lines * (2 * row_len) ** 2
    own_lines, sent_lines = call(
        "coil_forward",
        coil_forward_body,
        [jax.ShapeDtypeStruct(line_shape, F32), jax.ShapeDtypeStruct(line_shape, BF16)],
        (grad_now, sens, high, low),
        "VHHH",
        scratch=scratch,
        flops=coil_flops,
        nbytes=4000000,
    )
    own_slices = [lax.dynamic_index_in_dim(features[0], pick(j), 0, keepdims=False) for j in order]
    full_in, main_in, corner_in, ends_in = halo(own_slices)
    sent_lines, _ = lax.optimization_barrier((sent_lines, full_in[depth_len : 2 * depth_len]))
    other_lines = [
        lax.ppermute(sent_lines, "slab", [(i, (i + k) % slabs) for i in range(slabs)]) for k in range(1, slabs)
    ]
    spread = -(projection[:, None, None, :] * jnp.eye(col_len, dtype=BF16)[None, :, :, None])
    spread = spread.reshape(2 * col_len, packed_len)
    spread = jnp.concatenate([spread] * 3, axis=0)

    bands = [pltpu.VMEM((len(g[0]) * LANES, 3 * LANES), BF16) for g in corner_groups]

    conv_flops = 2 * row_len * len(main_entries) * packed_len * 3 * depth_len * LANES
    small_flops = 2 * row_len * 2 * packed_len * 3 * LANES

    def conv_main(name, back, inputs, after=(), stacked=()):
        return call(
            name,
            functools.partial(conv_main_body, main_entries, flip, back, stacked),
            [jax.ShapeDtypeStruct(slab_shape, F32)]
            + [jax.ShapeDtypeStruct((len(stacked) * LANES, packed_len // LANES * row_len), BF16)] * bool(stacked),
            (scal, conv_weight, *inputs),
            "SV" + "V" * len(inputs),
            scratch=[pltpu.VMEM((len(main_entries) * LANES, 3 * depth_len * LANES), BF16)],
            flops=conv_flops,
            nbytes=5000000,
            after=after,
        )

    whole = tuple(range(3 * depth_len))
    acc, stack_full = conv_main("conv_act", False, main_in, (), whole)
    grad_image = call(
        "coil_back",
        functools.partial(coil_backward_body, slabs),
        jax.ShapeDtypeStruct(grad_now.shape, F32),
        (grad_now, sens, mask[0], high, low, own_lines, *other_lines),
        "VVVVVV" + "V" * len(other_lines),
        after=[acc],
        scratch=scratch,
        flops=coil_flops,
        nbytes=5000000,
    )

    grad_outs = call(
        "grad_act",
        functools.partial(grad_act_body, corner_groups, flip),
        [pltpu.VMEM(slice_shape, BF16)] * depth_len
        + [pltpu.VMEM((3 * LANES, packed_len // LANES * row_len), BF16)] * len(edges),
        (scal, acc, grad_image, spread, conv_weight, *[values[0] for values in ends_in], *corner_in),
        "SVHVV" + "V" * (len(edges) + len(corner_in)),
        flops=small_flops,
        nbytes=4000000,
        scratch=bands,
        after=[],
    )

    grad_act, stack_ends = grad_outs[:depth_len], grad_outs[depth_len:]
    _, main_grad, corner_grad, _ = halo(grad_act)

    share = (taps + 1) // 2 * channels // 2
    stacks = [stack_full, *stack_ends]
    weight_groups = [[(kind, j) for kind in ("own", "on", "off") for j in order]]
    weight_groups += [[(kind, edge[1]) for kind in ("own", "off", "on")] for edge in edges]
    keep, send = call(
        "grad_weight",
        functools.partial(grad_weight_body, weight_groups, tuple(order), flip),
        [jax.ShapeDtypeStruct((share, LANES), F32)] * 2,
        (scal, *stacks, *grad_act),
        "SV" + "M" * (len(stacks) - 1 + depth_len),
        after=[],
        scratch=[
            pltpu.VMEM((packed_len // LANES * row_len, 3 * depth_len * LANES), BF16),
            pltpu.VMEM((2 * share, LANES), F32),
        ],
        flops=conv_flops,
        nbytes=5000000,
    )

    (acc_back,) = conv_main("conv_back", True, main_grad)
    pieces, spots, late = sum_over_mesh(keep, send, phases, slabs, [acc_back])
    for k in range(len(edges)):
        value, _ = lax.optimization_barrier((main_grad[3 * depth_len + k], late))
        corner_grad[2 * k + 1] = pass_phase(value, on)
    grad_features, grad_weight = call(
        "finish_both",
        functools.partial(final_body, corner_groups, flip),
        [jax.ShapeDtypeStruct(slab_shape, BF16), jax.ShapeDtypeStruct(conv_weight.shape, F32)],
        (scal, acc_back, conv_weight, *corner_grad, spots, *pieces),
        "SVV" + "V" * len(corner_grad) + "S" + "V" * len(pieces),
        scratch=bands + [pltpu.VMEM((len(pieces),) + pieces[0].shape, F32)],
        flops=small_flops,
        nbytes=4000000,
    )
    return (grad_image[None], grad_features[None], grad_weight)


def solution(mesh):
    in_specs = (
        P("phase", "slab", None, None),
        P(),
        P(),
        P("phase", "slab", None, None, None),
        P("slab", None, None, None, None),
        P("phase", None, None),
    )
    out_specs = (P("phase", "slab", None, None, None), P("phase", "slab", None, None), P())
    body = functools.partial(local, mesh.shape["phase"], mesh.shape["slab"])
    return jax.shard_map(body, mesh=mesh, in_specs=in_specs, out_specs=out_specs, check_vma=False)
```

```python
import functools
import math

import jax
import jax.numpy as jnp
import ml_dtypes
import numpy as np
from jax import lax
from jax.experimental import pallas as pl
from jax.experimental.pallas import tpu as pltpu
from jax.sharding import PartitionSpec as P

F32, BF16 = jnp.float32, jnp.bfloat16
VMEM = pl.BlockSpec(memory_space=pltpu.VMEM)
SMEM = pl.BlockSpec(memory_space=pltpu.SMEM)
LIMIT = 32 * 1024 * 1024
LANES = 128


ANY = pl.BlockSpec(memory_space=pl.ANY)
SPECS = {"S": SMEM, "V": VMEM, "M": VMEM, "H": VMEM}


def call(name, body, outs, ins, kinds, scratch=(), flops=0, nbytes=0, after=()):
    count, waits = len(ins), len(after)

    def run(*refs):
        body(*refs[:count], *refs[count + waits :])

    spaces = {"M": pltpu.VMEM, "H": pltpu.HBM}
    ins = [
        pltpu.with_memory_space_constraint(x, spaces[kind]) if kind in spaces else x for x, kind in zip(ins, kinds)
    ]
    return pl.pallas_call(
        run,
        out_shape=outs,
        in_specs=[SPECS[kind] for kind in kinds] + [ANY] * waits,
        out_specs=[VMEM] * len(outs) if isinstance(outs, (list, tuple)) else VMEM,
        scratch_shapes=list(scratch),
        compiler_params=pltpu.CompilerParams(vmem_limit_bytes=LIMIT),
        cost_estimate=pl.CostEstimate(flops=flops, bytes_accessed=nbytes, transcendentals=0),
        name=name,
    )(*ins, *after)


def dft_packed(length):
    full = length // LANES * LANES
    part = np.concatenate([np.zeros(full), np.ones(full), np.zeros(length - full), np.ones(length - full)])
    index = np.concatenate([np.arange(full)] * 2 + [np.arange(full, length)] * 2)
    angle = (index[:, None] * index[None, :] % length) * (2.0 * math.pi / length)
    cosine, sine = np.cos(angle), np.sin(angle)
    same = part[:, None] == part[None, :]
    matrix = np.where(same, cosine, np.where(part[:, None] == 0, -sine, sine)) / math.sqrt(length)
    high = matrix.astype(ml_dtypes.bfloat16)
    low = (matrix - high.astype(np.float64)).astype(ml_dtypes.bfloat16)
    return high, low


def split(value):
    high = value.astype(BF16)
    return high, (value - high.astype(F32)).astype(BF16)


def dot3(high, low, mat_high, mat_low, dims):
    dot = functools.partial(lax.dot_general, dimension_numbers=(dims, ((), ())), preferred_element_type=F32)
    return dot(high, mat_high) + (dot(high, mat_low) + dot(low, mat_high))


def coil_forward_body(grad_ref, sens_ref, high_ref, low_ref, out_ref, send_ref, x_high, x_low):
    depth_len, coils, _, col_len, row_len = sens_ref.shape
    full = row_len // LANES * LANES
    count = coils * col_len
    for z in range(depth_len):
        sens_r, sens_i = sens_ref[z, :, 0], sens_ref[z, :, 1]
        img_r, img_i = grad_ref[z, 0][None], grad_ref[z, 1][None]
        real = sens_r * img_r - sens_i * img_i
        imag = sens_r * img_i + sens_i * img_r
        rest = jnp.concatenate([real[..., full:], imag[..., full:]], axis=-1)
        for piece, start in ((real[..., :full], 0), (imag[..., :full], full), (rest, 2 * full)):
            width = piece.shape[-1]
            high, low = split(piece.reshape(count, width))
            x_high[z * count : (z + 1) * count, start : start + width] = high
            x_low[z * count : (z + 1) * count, start : start + width] = low
    result = dot3(x_high[...], x_low[...], high_ref[...], low_ref[...], ((1,), (0,)))
    out_ref[...] = result
    send_ref[...] = result.astype(BF16)


def coil_backward_body(slabs, grad_ref, sens_ref, mask_ref, high_ref, low_ref, own_ref, *refs):
    others, out_ref, x_high, x_low = refs[: slabs - 1], refs[-3], refs[-2], refs[-1]
    depth_len, coils, _, col_len, row_len = sens_ref.shape
    total = slabs * depth_len
    full = row_len // LANES * LANES
    rem = row_len - full
    count = coils * col_len
    mask = mask_ref[...].astype(F32)

    def table(turn):
        real = jnp.zeros((1, row_len), F32)
        imag = jnp.zeros((1, row_len), F32)
        has_imag = False
        for kz in range(total):
            angle = 2.0 * math.pi * ((kz * turn) % total) / total
            cosine, sine = round(math.cos(angle), 15) / total, round(math.sin(angle), 15) / total
            real = real + mask[kz : kz + 1] * cosine
            if sine != 0.0:
                imag = imag + mask[kz : kz + 1] * sine
                has_imag = True
        real_rest = jnp.concatenate([real[:, full:], real[:, full:]], axis=-1)
        imag_rest = jnp.concatenate([-imag[:, full:], imag[:, full:]], axis=-1)
        return real[:, :full], imag[:, :full], real_rest, imag_rest, has_imag

    tables = {}
    for z in range(depth_len):
        sums = None
        for step in range(slabs):
            src = own_ref if step == 0 else others[step - 1]
            for zin in range(depth_len):
                turn = (step * depth_len + z - zin) % total
                if turn not in tables:
                    tables[turn] = table(turn)
                real, imag, real_rest, imag_rest, has_imag = tables[turn]
                block = src[zin * count : (zin + 1) * count, :].astype(F32)
                v_r, v_i, v_rest = block[:, :full], block[:, full : 2 * full], block[:, 2 * full :]
                if has_imag:
                    terms = (
                        real * v_r - imag * v_i,
                        real * v_i + imag * v_r,
                        real_rest * v_rest + imag_rest * pltpu.roll(v_rest, rem, 1),
                    )
                else:
                    terms = (real * v_r, real * v_i, real_rest * v_rest)
                sums = terms if sums is None else tuple(a + b for a, b in zip(sums, terms))
        for piece, start in zip(sums, (0, full, 2 * full)):
            high, low = split(piece)
            x_high[z * count : (z + 1) * count, start : start + piece.shape[1]] = high
            x_low[z * count : (z + 1) * count, start : start + piece.shape[1]] = low
    back = dot3(x_high[...], x_low[...], high_ref[...], low_ref[...], ((1,), (1,)))
    for z in range(depth_len):
        sens_r, sens_i = sens_ref[z, :, 0], sens_ref[z, :, 1]
        block = back[z * count : (z + 1) * count].reshape(coils, col_len, 2 * row_len)
        b_r, b_i, b_rest = block[..., :full], block[..., full : 2 * full], block[..., 2 * full :]
        s_r, s_i = sens_r[..., :full], sens_i[..., :full]
        out_ref[z, 0, :, :full] = grad_ref[z, 0, :, :full] - jnp.sum(s_r * b_r + s_i * b_i, axis=0)
        out_ref[z, 1, :, :full] = grad_ref[z, 1, :, :full] - jnp.sum(s_r * b_i - s_i * b_r, axis=0)
        s_rest = jnp.concatenate([sens_r[..., full:], sens_i[..., full:]], axis=-1)
        turned = pltpu.roll(b_rest, rem, 2)
        along = jnp.sum(s_rest * b_rest, axis=0)
        across = jnp.sum(s_rest * turned, axis=0)
        real = along + pltpu.roll(along, rem, 1)
        imag = across - pltpu.roll(across, rem, 1)
        out_ref[z, 0, :, full:] = grad_ref[z, 0, :, full:] - real[:, :rem]
        out_ref[z, 1, :, full:] = grad_ref[z, 1, :, full:] - imag[:, :rem]


def tap_group(scal_ref, phase_kind, flip, step_z):
    core = scal_ref[1]
    time_off = {"own": 1, "on": 2 - 2 * core, "off": 2 * core}[phase_kind]
    depth_off = jnp.where(scal_ref[0] == 1, 2 - step_z, step_z) if flip else step_z
    return 9 * time_off + 3 * depth_off


def shift_rows(value, step):
    rows = value.shape[0]
    turned = pltpu.roll(value, step % rows, 0)
    place = lax.broadcasted_iota(jnp.int32, value.shape, 0)
    return jnp.where(place == (0 if step > 0 else rows - 1), 0.0, turned)


def two_columns(weight):
    zero = jnp.zeros_like(weight)
    return jnp.concatenate(
        [jnp.concatenate([weight, zero], axis=1), jnp.concatenate([zero, weight], axis=1)], axis=0
    ).astype(BF16)


def fill_band(scal_ref, weight_ref, band, entries, outs, flip, back):
    width = LANES * len(outs)
    made = {}
    for i, (kind, place) in enumerate(entries):
        for j, out_place in enumerate(outs):
            step_z = place - out_place + 1
            for dy in range(3):
                lanes = slice(dy * width + j * LANES, dy * width + (j + 1) * LANES)
                if 0 <= step_z <= 2:
                    if (kind, step_z, dy) not in made:
                        tap = tap_group(scal_ref, kind, flip, step_z) + dy
                        weight = weight_ref[weight_ref.shape[0] - 1 - tap if back else tap].astype(F32)
                        made[kind, step_z, dy] = two_columns(weight.T if back else weight)
                    block = made[kind, step_z, dy]
                else:
                    block = jnp.zeros((LANES, LANES), BF16)
                band[i * LANES : (i + 1) * LANES, lanes] = block


def place_of(scal_ref, j, depth_len, flip):
    return jnp.where(scal_ref[0] == 1, depth_len - 1 - j, j) if flip else j


def conv_columns(refs, band, lanes):
    stacked = jnp.concatenate([ref[:, lanes] for ref in refs], axis=1)
    taps = jnp.dot(stacked, band[...], preferred_element_type=F32)
    width = taps.shape[1] // 3
    return (
        shift_rows(taps[:, :width], 1)
        + taps[:, width : 2 * width]
        + shift_rows(taps[:, 2 * width :], -1)
    )


def stack_body(*refs):
    inputs, out_ref = refs[:-1], refs[-1]
    rows, packed_len = inputs[0].shape
    for i, start in enumerate(range(0, packed_len, 2 * LANES)):
        for k, ref in enumerate(inputs):
            pair = jnp.concatenate([ref[:, start : start + LANES], ref[:, start + LANES : start + 2 * LANES]], axis=0)
            value = pair.astype(F32).T
            out_ref[k * LANES : (k + 1) * LANES, 2 * rows * i : 2 * rows * (i + 1)] = value.astype(BF16)


def conv_main_body(entries, flip, back, stacked, scal_ref, weight_ref, *refs):
    inputs, out_ref, band = refs[: len(entries)], refs[len(entries)], refs[-1]
    if stacked:
        stack_body(*[inputs[k] for k in stacked], refs[len(entries) + 1])
    depth_len = out_ref.shape[0]
    fill_band(scal_ref, weight_ref, band, entries, tuple(range(depth_len)), flip, back)
    for start in range(0, out_ref.shape[2], LANES):
        lanes = slice(start, start + LANES)
        result = conv_columns(inputs, band, lanes)
        for j in range(depth_len):
            out_ref[j, :, lanes] = result[:, j * LANES : (j + 1) * LANES]


def corner_plans(groups, flip, back, scal_ref, weight_ref, inputs, bands):
    plans = {}
    for (entries, out_place), band in zip(groups, bands):
        fill_band(scal_ref, weight_ref, band, entries, (out_place,), flip, back)
        plans[out_place] = (inputs[: len(entries)], band)
        inputs = inputs[len(entries) :]
    return plans


def grad_act_body(groups, flip, scal_ref, acc_ref, image_ref, spread_ref, weight_ref, *refs):
    depth_len, count = acc_ref.shape[0], len(groups)
    slab_in, inputs, refs = refs[:count], refs[count : 3 * count], refs[3 * count :]
    outs, ends, bands = refs[:depth_len], refs[depth_len : depth_len + count], refs[depth_len + count :]
    for k, end in enumerate(ends):
        stack_body(slab_in[k], *inputs[2 * k : 2 * k + 2], end)
    plans = corner_plans(groups, flip, False, scal_ref, weight_ref, inputs, bands)
    row_len = image_ref.shape[3]
    for j in range(depth_len):
        place = place_of(scal_ref, j, depth_len, flip)
        image = image_ref[place].reshape(-1, row_len)
        first, low = split(image)
        middle, last = split(image - first.astype(F32))
        stacked = jnp.concatenate([first, middle, last], axis=0)
        for start in range(0, acc_ref.shape[2], LANES):
            lanes = slice(start, start + LANES)
            grad_silu = lax.dot_general(
                stacked, spread_ref[:, lanes], (((0,), (0,)), ((), ())), preferred_element_type=F32
            )
            act = acc_ref[j, :, lanes]
            if j in plans:
                act = act + conv_columns(*plans[j], lanes)
            gate = 0.5 * jnp.tanh(0.5 * act) + 0.5
            outs[j][:, lanes] = (grad_silu * (gate * (1.0 + act * (1.0 - gate)))).astype(BF16)


def grad_feature_body(groups, flip, scal_ref, acc_ref, weight_ref, *refs):
    inputs, out_ref, bands = refs[: 2 * len(groups)], refs[2 * len(groups)], refs[2 * len(groups) + 1 :]
    plans = corner_plans(groups, flip, True, scal_ref, weight_ref, inputs, bands)
    depth_len = acc_ref.shape[0]
    for j in range(depth_len):
        place = jnp.where(scal_ref[0] == 1, depth_len - 1 - j, j) if flip else j
        for start in range(0, acc_ref.shape[2], LANES):
            lanes = slice(start, start + LANES)
            total = acc_ref[j, :, lanes]
            if j in plans:
                total = total + conv_columns(*plans[j], lanes)
            out_ref[place, :, lanes] = total.astype(BF16)


def reach(place, outs):
    return [j for j, out_place in enumerate(outs) if 0 <= place - out_place + 1 <= 2]


def grad_weight_body(groups, outs, flip, scal_ref, *refs):
    n_out = len(outs)
    keep_ref, send_ref, right, packed = refs[-4:]
    stacks, grads = refs[: -4 - n_out], refs[-4 - n_out : -4]
    rows, packed_len = grads[0].shape
    half = LANES // 2
    width = 3 * LANES
    for i, start in enumerate(range(0, packed_len, LANES)):
        lanes = slice(start, start + LANES)
        span = slice(i * rows, (i + 1) * rows)
        for j, ref in enumerate(grads):
            value = ref[:, lanes].astype(F32)
            at = j * width
            right[span, at : at + LANES] = shift_rows(value, -1).astype(BF16)
            right[span, at + LANES : at + 2 * LANES] = ref[:, lanes]
            right[span, at + 2 * LANES : at + 3 * LANES] = shift_rows(value, 1).astype(BF16)
    entries, rows_of = [], []
    for stack, group in zip(stacks, groups):
        near = reach(group[0][1], outs)
        part = jnp.dot(
            stack[...], right[:, near[0] * width : (near[-1] + 1) * width], preferred_element_type=F32
        )
        for k, entry in enumerate(group):
            entries.append(entry)
            rows_of.append({
                j: part[k * LANES : (k + 1) * LANES, (j - near[0]) * width : (j - near[0] + 1) * width] for j in near
            })
    quarter = half // 2
    lane = lax.broadcasted_iota(jnp.int32, (quarter, LANES), 1)
    packed[27 * quarter :] = jnp.zeros((packed.shape[0] - 27 * quarter, LANES), F32)
    for kind in ("own", "on", "off"):
        for step_z in range(3):
            for dy in range(3):
                total = None
                for k, (this, place) in enumerate(entries):
                    for j, out_place in enumerate(outs):
                        if this == kind and place - out_place + 1 == step_z:
                            block = rows_of[k][j][:, dy * LANES : (dy + 1) * LANES]
                            total = block if total is None else total + block
                direct = jnp.where(lane < half, total[:quarter], total[3 * quarter :])
                turned = jnp.where(lane < half, total[quarter : 2 * quarter], total[2 * quarter : 3 * quarter])
                tap = tap_group(scal_ref, kind, flip, step_z) + dy
                packed[pl.ds(pl.multiple_of(tap * quarter, quarter), quarter), :] = direct + pltpu.roll(turned, half, 1)
    share = packed.shape[0] // 2
    core = scal_ref[1]
    keep_ref[...] = packed[pl.ds(pl.multiple_of(core * share, quarter), share), :]
    send_ref[...] = packed[pl.ds(pl.multiple_of((1 - core) * share, quarter), share), :]


def unpack_body(where_ref, *refs):
    pieces, out_ref, packed = refs[:-2], refs[-2], refs[-1]
    share = pieces[0].shape[0]
    for i, ref in enumerate(pieces):
        packed[where_ref[i]] = ref[...].astype(F32)
    flat = packed[...].reshape(-1, LANES)
    taps, height, _ = out_ref.shape
    quarter = height // 2
    for tap in range(taps):
        block = flat[tap * quarter : (tap + 1) * quarter]
        out_ref[tap, :quarter, :] = block[:, : LANES // 2]
        out_ref[tap, quarter:, :] = pltpu.roll(block, LANES // 2, 1)[:, : LANES // 2]


def final_body(groups, flip, scal_ref, acc_ref, weight_ref, *refs):
    corners, count = refs[: 2 * len(groups)], 2 * len(groups)
    where_ref, pieces = refs[count], refs[count + 1 : count + 5]
    features_ref, taps_ref, packed, bands = refs[count + 5], refs[count + 6], refs[-1], refs[count + 7 : -1]
    unpack_body(where_ref, *pieces, taps_ref, packed)
    grad_feature_body(groups, flip, scal_ref, acc_ref, weight_ref, *corners, features_ref, *bands)


def pair_on(size):
    return [(i, i ^ 1) for i in range(size)]


def pair_off(size):
    return [(i, (i - 1) % size if i % 2 == 0 else (i + 1) % size) for i in range(size)]


def fold_body(pick_ref, keep_ref, got_ref, own_ref, send_ref):
    rows = own_ref.shape[0]
    for spot, out_ref in ((pick_ref[0], own_ref), (1 - pick_ref[0], send_ref)):
        span = pl.ds(pl.multiple_of(spot * rows, rows), rows)
        out_ref[...] = keep_ref[span, :] + got_ref[span, :]


def round_body(value_ref, got_ref, out_ref):
    out_ref[...] = (value_ref[...] + got_ref[...]).astype(out_ref.dtype)


def exchanges(axis, stride, size, total):
    return [(axis, [(i, i ^ (stride * bit)) for i in range(total)]) for bit in (1 << k for k in range(size.bit_length() - 1))]


def sum_over_mesh(keep, send, phases, slabs, after_finish):
    phase = lax.axis_index("phase")
    core, column = phase % 2, phase // 2 % 2
    part_shape = (keep.shape[0] // 2, LANES)
    across = [(p, p ^ 2) for p in range(phases)]
    part, other = call(
        "fold",
        fold_body,
        [jax.ShapeDtypeStruct(part_shape, F32)] * 2,
        (column.reshape(1), keep, lax.ppermute(send, "phase", pair_on(phases))),
        "SVV",
        nbytes=100000,
    )
    part = part + lax.ppermute(other, "phase", across)
    steps = exchanges("slab", 1, slabs, slabs) + exchanges("phase", 4, phases // 4, phases)
    for axis, perm in steps[:-1]:
        part = part + lax.ppermute(part, axis, perm)
    late = part
    axis, perm = steps[-1]
    part = call(
        "finish",
        round_body,
        jax.ShapeDtypeStruct(part_shape, BF16),
        (part, lax.ppermute(part, axis, perm)),
        "VV",
        nbytes=30000,
        after=after_finish,
    )
    pieces = [part, lax.ppermute(part, "phase", across)]
    pieces += [lax.ppermute(piece, "phase", pair_on(phases)) for piece in pieces]
    spots = [2 * core + column, 2 * core + 1 - column]
    spots += [2 * (1 - core) + column, 2 * (1 - core) + 1 - column]
    return pieces, jnp.stack(spots).astype(jnp.int32), late


def local(phases, slabs, features, conv_weight, projection, grad_out, sens, mask):
    _, depth_len, row_len, packed_len = features.shape
    channels = conv_weight.shape[1]
    col_len = packed_len // channels
    coils = sens.shape[1]
    taps = conv_weight.shape[0]
    slab, core = lax.axis_index("slab"), lax.axis_index("phase") % 2
    flip = slabs == 2
    scal = jnp.stack([slab, core]).astype(jnp.int32)
    on, off = pair_on(phases), pair_off(phases)

    def pass_phase(value, perm):
        return lax.ppermute(value, "phase", perm)

    if flip:
        order = list(range(depth_len))
        edges = [(depth_len - 1, depth_len, [(0, 1), (1, 0)])]
        pick = lambda j: jnp.where(slab == 1, depth_len - 1 - j, j)
    else:
        order = list(range(depth_len))
        up = [(i, i + 1) for i in range(slabs - 1)]
        edges = [(depth_len - 1, -1, up), (0, depth_len, [(j, i) for i, j in up])]
        pick = lambda j: j

    first_sent = [edge[0] for edge in edges]

    def halo(own):
        off_in = {}
        for j in first_sent + [j for j in order if j not in first_sent]:
            off_in[j] = pass_phase(own[j], off)
        slab_in = [lax.ppermute(own[edge[0]], "slab", edge[2]) for edge in edges]
        on_in = [pass_phase(own[j], on) for j in order]
        corner_off = [lax.ppermute(off_in[edge[0]], "slab", edge[2]) for edge in edges]
        corner_on = [pass_phase(value, on) for value in slab_in]
        corners = []
        for a, b in zip(corner_off, corner_on):
            corners += [a, b]
        full = list(own) + on_in + [off_in[j] for j in order]
        ends = [list(values) for values in zip(slab_in, corner_off, corner_on)]
        return full, full + slab_in, corners, ends

    main_entries = (
        [(kind, j) for kind in ("own", "on", "off") for j in order] + [("own", edge[1]) for edge in edges]
    )
    corner_entries = []
    corner_groups = []
    for edge in edges:
        near = min(max(edge[1], 0), depth_len - 1)
        corner_groups.append(([("off", edge[1]), ("on", edge[1])], near))
        corner_entries += [("off", edge[1]), ("on", edge[1])]
    corner_groups.sort(key=lambda g: g[1])

    high, low = dft_packed(row_len)
    high, low = jnp.asarray(high), jnp.asarray(low)
    lines = depth_len * coils * col_len
    grad_now = grad_out[0]
    line_shape = (lines, 2 * row_len)
    slice_shape = (row_len, packed_len)
    slab_shape = (depth_len, row_len, packed_len)
    scratch = [pltpu.VMEM(line_shape, BF16)] * 2
    coil_flops = 3 * 2 * lines * (2 * row_len) ** 2
    own_lines, sent_lines = call(
        "coil_forward",
        coil_forward_body,
        [jax.ShapeDtypeStruct(line_shape, F32), jax.ShapeDtypeStruct(line_shape, BF16)],
        (grad_now, sens, high, low),
        "VHHH",
        scratch=scratch,
        flops=coil_flops,
        nbytes=4000000,
    )
    own_slices = [lax.dynamic_index_in_dim(features[0], pick(j), 0, keepdims=False) for j in order]
    full_in, main_in, corner_in, ends_in = halo(own_slices)
    sent_lines, _ = lax.optimization_barrier((sent_lines, full_in[depth_len : 2 * depth_len]))
    other_lines = [
        lax.ppermute(sent_lines, "slab", [(i, (i + k) % slabs) for i in range(slabs)]) for k in range(1, slabs)
    ]
    spread = -(projection[:, None, None, :] * jnp.eye(col_len, dtype=BF16)[None, :, :, None])
    spread = spread.reshape(2 * col_len, packed_len)
    spread = jnp.concatenate([spread] * 3, axis=0)

    bands = [pltpu.VMEM((len(g[0]) * LANES, 3 * LANES), BF16) for g in corner_groups]

    conv_flops = 2 * row_len * len(main_entries) * packed_len * 3 * depth_len * LANES
    small_flops = 2 * row_len * 2 * packed_len * 3 * LANES

    def conv_main(name, back, inputs, after=(), stacked=()):
        return call(
            name,
            functools.partial(conv_main_body, main_entries, flip, back, stacked),
            [jax.ShapeDtypeStruct(slab_shape, F32)]
            + [jax.ShapeDtypeStruct((len(stacked) * LANES, packed_len // LANES * row_len), BF16)] * bool(stacked),
            (scal, conv_weight, *inputs),
            "SV" + "V" * len(inputs),
            scratch=[pltpu.VMEM((len(main_entries) * LANES, 3 * depth_len * LANES), BF16)],
            flops=conv_flops,
            nbytes=5000000,
            after=after,
        )

    whole = tuple(range(3 * depth_len))
    acc, stack_full = conv_main("conv_act", False, main_in, (), whole)
    grad_image = call(
        "coil_back",
        functools.partial(coil_backward_body, slabs),
        jax.ShapeDtypeStruct(grad_now.shape, F32),
        (grad_now, sens, mask[0], high, low, own_lines, *other_lines),
        "VVVVVV" + "V" * len(other_lines),
        after=[acc],
        scratch=scratch,
        flops=coil_flops,
        nbytes=5000000,
    )

    grad_outs = call(
        "grad_act",
        functools.partial(grad_act_body, corner_groups, flip),
        [pltpu.VMEM(slice_shape, BF16)] * depth_len
        + [pltpu.VMEM((3 * LANES, packed_len // LANES * row_len), BF16)] * len(edges),
        (scal, acc, grad_image, spread, conv_weight, *[values[0] for values in ends_in], *corner_in),
        "SVHVV" + "V" * (len(edges) + len(corner_in)),
        flops=small_flops,
        nbytes=4000000,
        scratch=bands,
        after=[],
    )

    grad_act, stack_ends = grad_outs[:depth_len], grad_outs[depth_len:]
    _, main_grad, corner_grad, _ = halo(grad_act)

    share = (taps + 1) // 2 * channels // 2
    stacks = [stack_full, *stack_ends]
    weight_groups = [[(kind, j) for kind in ("own", "on", "off") for j in order]]
    weight_groups += [[(kind, edge[1]) for kind in ("own", "off", "on")] for edge in edges]
    keep, send = call(
        "grad_weight",
        functools.partial(grad_weight_body, weight_groups, tuple(order), flip),
        [jax.ShapeDtypeStruct((share, LANES), F32)] * 2,
        (scal, *stacks, *grad_act),
        "SV" + "M" * (len(stacks) - 1 + depth_len),
        after=[],
        scratch=[
            pltpu.VMEM((packed_len // LANES * row_len, 3 * depth_len * LANES), BF16),
            pltpu.VMEM((2 * share, LANES), F32),
        ],
        flops=conv_flops,
        nbytes=5000000,
    )

    (acc_back,) = conv_main("conv_back", True, main_grad)
    pieces, spots, late = sum_over_mesh(keep, send, phases, slabs, [acc_back])
    for k in range(len(edges)):
        value, _ = lax.optimization_barrier((main_grad[3 * depth_len + k], late))
        corner_grad[2 * k + 1] = pass_phase(value, on)
    grad_features, grad_weight = call(
        "finish_both",
        functools.partial(final_body, corner_groups, flip),
        [jax.ShapeDtypeStruct(slab_shape, BF16), jax.ShapeDtypeStruct(conv_weight.shape, F32)],
        (scal, acc_back, conv_weight, *corner_grad, spots, *pieces),
        "SVV" + "V" * len(corner_grad) + "S" + "V" * len(pieces),
        scratch=bands + [pltpu.VMEM((len(pieces),) + pieces[0].shape, F32)],
        flops=small_flops,
        nbytes=4000000,
    )
    return (grad_image[None], grad_features[None], grad_weight)


def solution(mesh):
    in_specs = (
        P("phase", "slab", None, None),
        P(),
        P(),
        P("phase", "slab", None, None, None),
        P("slab", None, None, None, None),
        P("phase", None, None),
    )
    out_specs = (P("phase", "slab", None, None, None), P("phase", "slab", None, None), P())
    body = functools.partial(local, mesh.shape["phase"], mesh.shape["slab"])
    return jax.shard_map(body, mesh=mesh, in_specs=in_specs, out_specs=out_specs, check_vma=False)
```
